128 devices in a mesh: grp: 2 (over core), dp: 16 (over y, z), sp: 4 (over x).
Axes of the slice: x: 4, y: 4, z: 4, core: 2. Of those that a mesh axis runs over, the one named last changes fastest.
Arguments:
- tokens: bfloat16 [16384, 7168], P(('grp', 'dp', 'sp')), may hold values from -6 to 6
- grad_out: bfloat16 [16384, 7168], P(('grp', 'dp', 'sp')), may hold values from -6 to 6
- expert_ids: int32 [16384, 8], P(('grp', 'dp', 'sp')), may hold values from 0 to 255, all different within a row; in each aligned block of 128 rows (0 to 127, 128 to 255, ...) at most 6 rows name the same one
- gate_codes: int32 [16384, 8], P(('grp', 'dp', 'sp')), may hold values from 1 to 4095
- lengths: int32 [128, 2], P(('grp', 'dp', 'sp')), may hold values from 1 to 64, 96 in all within a row
- w_gate: bfloat16 [8, 7168, 2048], P(('grp', 'sp'), None, 'dp'), may hold values from -0.0625 to 0.0625
- w_up: bfloat16 [8, 7168, 2048], P(('grp', 'sp'), None, 'dp'), may hold values from -0.0625 to 0.0625
- w_down: bfloat16 [8, 2048, 7168], P(('grp', 'sp'), 'dp'), may hold values from -0.125 to 0.125
Outputs:
- grad_tokens: bfloat16 [16384, 7168], P(('grp', 'dp', 'sp'))
- grad_gate_w: bfloat16 [8, 7168, 2048], P(('grp', 'sp'), None, 'dp')
- grad_up_w: bfloat16 [8, 7168, 2048], P(('grp', 'sp'), None, 'dp')
- grad_down_w: bfloat16 [8, 2048, 7168], P(('grp', 'sp'), 'dp')
The draws below stay inside these ranges and needn't reach their ends.
Inputs may be any that keep to these rules, and one draw needn't show every extreme that they name: `expert_ids`: each row names 8 different experts; no expert is named by more than 6 rows of one device. The 2 lengths of one device sum to 96.
All inputs are finite; a program needn't handle non-finite values.
Results may differ from the reference program's by a relative error of at most 0.019.
Values may be sent and summed in bfloat16 or wider, within the bound.
No kernel may reach another device: no remote copies, remote signals or barrier semaphores. Data moves between devices by JAX's collectives and lax.ppermute only.
A program may use at most 192 MiB of HBM per device.

```python
import math
import jax
import jax.numpy as jnp
import numpy as np
from jax import lax

D = 7168
FF = 2048
ALL_EXPERTS = 256
TOPK = 8
TOK_DEV = 128
SEQ_DEV = 2
SLOT = 64
LIVE = 96
CAP = 6
EXPERTS = 8
TOKENS = 16384
N_DP = 16
DEVICES = 128


def touch_ends(array, rng, low, high):
    index_at = [jax.random.randint(jax.random.fold_in(rng, axis), (), 0, length) for axis, length in enumerate(array.shape)]
    longest = array.shape.index(max(array.shape))
    next_to = index_at[:longest] + [(index_at[longest] + 1) % array.shape[longest]] + index_at[longest + 1:]
    return array.at[tuple(index_at)].set(low).at[tuple(next_to)].set(high)


def level_of(rng, extent, split, smallest, high):
    loudness, own = 1.0, jax.random.fold_in(rng, 6)
    for dim, parts in split:
        draws = jnp.exp(jax.random.uniform(jax.random.fold_in(own, dim), (parts,), jnp.float32, smallest / len(split), high / len(split)))
        loudness = loudness * jnp.repeat(draws, extent[dim] // parts).reshape([-1 if axis == dim else 1 for axis in range(len(extent))])
    return loudness


def length_profile(number_of, total, limit, lean):
    weights = [(1 << 20) // math.isqrt(rank ** lean) + 1 for rank in range(2, number_of + 1)]
    surplus, counts = total - limit - (number_of - 1), [1] * (number_of - 1)
    while surplus > 0:
        candidates = [i for i in range(number_of - 1) if counts[i] < limit]
        pool, budget = sum([weights[i] for i in candidates]), surplus
        for i in candidates:
            addition = min(limit - counts[i], max(1, budget * weights[i] // pool), surplus)
            counts[i] = counts[i] + addition
            surplus = surplus - addition
    return np.array([limit] + counts)


def uneven_parts(stream_key, number_of, total, limit, slope):
    if number_of == 2:
        one = jax.random.randint(stream_key, (), max(1, total - limit), min(limit, total - 1) + 1)
        return jnp.stack([one, total - one])
    sizes = jnp.asarray(length_profile(number_of, total, limit, slope), jnp.int32)
    pairs = (number_of - 1) // 2
    donor, receiver = sizes[1:1 + 2 * pairs:2], sizes[2:2 + 2 * pairs:2]
    margin = jnp.minimum(donor - 1, limit - receiver)
    moved = jax.random.randint(jax.random.fold_in(stream_key, 1), (pairs,), 0, 1 << 20) % (margin + 1)
    sizes = sizes.at[1:1 + 2 * pairs:2].set(donor - moved).at[2:2 + 2 * pairs:2].set(receiver + moved)
    return sizes[jax.random.permutation(jax.random.fold_in(stream_key, 2), number_of)]


def assign_block(stream_key, own, number, rows, number_of, top, limit, slope):
    order = jax.random.permutation(stream_key, number_of)
    packed, usual = portions_of(number_of, rows * top, limit, slope, True), portions_of(number_of, rows * top, limit, slope, False)
    places = jnp.arange(number_of)

    def named(sizes, offset_by):
        used = int((sizes > 0).sum())
        fixed = max(1, used // 4)
        shifted = fixed + (places - fixed + offset_by * (used - fixed)) % max(1, number_of - fixed)
        return jnp.zeros((number_of,), jnp.int32).at[order[jnp.where(places < fixed, places, shifted)]].set(jnp.asarray(sizes, jnp.int32))

    sizes = jnp.where(number % 4 == 0, named(packed, number // 4), named(usual, number - number // 4 - 1))
    mixed = jax.random.permutation(jax.random.fold_in(own, 3), number_of)
    source_of, sink = mixed[0:number_of // 2 * 2:2], mixed[1:number_of // 2 * 2:2]
    room = jnp.minimum(sizes[source_of] - 1, limit - sizes[sink]) // 2
    room = jnp.where((source_of == order[0]) | (sink == order[0]) | (sizes[sink] == 0), 0, jnp.maximum(room, 0))
    shifted = jax.random.randint(jax.random.fold_in(own, 4), (number_of // 2,), 0, 1 << 20) % (room + 1)
    sizes = sizes.at[source_of].add(-shifted).at[sink].add(shifted)
    members = jnp.searchsorted(jnp.cumsum(sizes), jnp.arange(rows * top), side="right").astype(jnp.int32)
    listing = members.reshape(top, rows).T
    listing = listing[jax.random.permutation(jax.random.fold_in(own, 1), rows)]
    offset_by = jax.random.randint(jax.random.fold_in(own, 2), (rows, 1), 0, top)
    return jnp.take_along_axis(listing, (jnp.arange(top)[None, :] + offset_by) % top, axis=1)


def portions_of(amount, total, bound, skew, full):
    loads = [(1 << 20) // math.isqrt(grade ** skew) + 1 for grade in range(1, amount + 1)]
    largest = bound if full else min(bound, max(-(-total // amount), total * loads[0] // sum(loads)))
    least = 1 if total - largest >= amount - 1 else 0
    counts, spare = [largest] + [least] * (amount - 1), total - largest - least * (amount - 1)
    while spare > 0:
        free = [i for i in range(1, amount) if counts[i] < largest] or [i for i in range(1, amount) if counts[i] < bound]
        whole, budget = sum([loads[i] for i in free]), spare
        for i in free:
            more = min(bound - counts[i], max(1, budget * loads[i] // whole), spare)
            counts[i] = counts[i] + more
            spare = spare - more
    return np.array(counts)


def noise(stream_key, shape, deviation, limit, cuts=(), held_as=jnp.bfloat16):
    result = jax.random.normal(stream_key, shape, jnp.float32) * deviation
    if len(cuts) > 0:
        result = level_of(stream_key, shape, cuts, -0.22, 0.18) * result
    return jnp.clip(result, min=-limit, max=limit).astype(held_as)


def setup_inputs(seed: int = 0) -> dict:
    key_of = jax.random.split(jax.random.key(seed), 9)
    tokens = noise(key_of[0], (TOKENS, D), 1.0, 6.0, ((0, 128),))
    grad_out = noise(key_of[1], (TOKENS, D), 1.0, 6.0, ((0, 128),))
    expert_ids_keys = jax.random.split(jax.random.fold_in(key_of[2], 1), TOKENS // TOK_DEV)
    expert_ids_turns = jax.random.permutation(jax.random.fold_in(key_of[2], 3), TOKENS // TOK_DEV)
    expert_ids = jax.vmap(lambda own, number: assign_block(jax.random.fold_in(key_of[2], 2), own, number, TOK_DEV, ALL_EXPERTS, TOPK, CAP, 2))(expert_ids_keys, expert_ids_turns).reshape((TOKENS, TOPK))
    gate_codes = touch_ends(jax.random.randint(key_of[3], (TOKENS, TOPK), 1, 4096), jax.random.fold_in(key_of[3], 1), 1, 4095).astype(jnp.int32)
    lengths = jax.vmap(lambda own: uneven_parts(own, SEQ_DEV, LIVE, SLOT, 1))(jax.random.split(key_of[4], DEVICES)).reshape((DEVICES, SEQ_DEV)).astype(jnp.int32)
    w_gate = noise(key_of[5], (EXPERTS, D, FF), D ** -0.5, 0.0625, ((0, 8), (2, 16)))
    w_up = noise(key_of[6], (EXPERTS, D, FF), D ** -0.5, 0.0625, ((0, 8), (2, 16)))
    w_down = noise(key_of[7], (EXPERTS, FF, D), FF ** -0.5, 0.125, ((0, 8), (1, 16)))
    return {"tokens": tokens, "grad_out": grad_out, "expert_ids": expert_ids, "gate_codes": gate_codes, "lengths": lengths, "w_gate": w_gate, "w_up": w_up, "w_down": w_down}


GRID_SCALE = 2048.0
HIGHEST = lax.Precision.HIGHEST


def slot_tables(expert_ids, gate_codes, lengths, experts):
    tok_count = expert_ids.shape[0]
    sample_count = lengths.shape[0]
    slot_len = tok_count // sample_count
    position = jnp.arange(tok_count, dtype=jnp.int32)
    sample_of = position // slot_len
    offset = position % slot_len
    samples = jnp.arange(sample_count, dtype=jnp.int32)
    length_here = jnp.sum(jnp.where(sample_of[:, None] == samples[None, :], lengths[None, :], 0), axis=1)
    is_live = offset < length_here
    expert_hit = expert_ids[:, :, None] == jnp.arange(experts, dtype=jnp.int32)[None, None, :]
    member = jnp.logical_and(jnp.any(expert_hit, axis=1), is_live[:, None]).astype(jnp.int32)
    gate_value = jnp.sum(jnp.where(expert_hit, gate_codes[:, :, None], 0), axis=1).astype(jnp.float32) / GRID_SCALE
    slot_rank = jnp.cumsum(member, axis=0, dtype=jnp.int32) - member
    slots = jnp.arange(CAP, dtype=jnp.int32)
    chosen = jnp.logical_and(slot_rank[None, :, :] == slots[:, None, None], member[None, :, :] > 0)
    select = jnp.transpose(chosen, (2, 0, 1)).astype(jnp.float32)
    slot_gate = jnp.einsum("ect,te->ec", select, gate_value, precision=HIGHEST)
    return select, slot_gate


def expert_pass(rows, grads, gate_w, up_w, down_w):
    gate_pre = jnp.dot(rows, gate_w, preferred_element_type=jnp.float32)
    up_pre = jnp.dot(rows, up_w, preferred_element_type=jnp.float32)
    logistic = jax.nn.sigmoid(gate_pre)
    hidden = (gate_pre * logistic * up_pre).astype(jnp.bfloat16)
    hidden_grad = lax.dot_general(grads, down_w, (((1,), (1,)), ((), ())), preferred_element_type=jnp.float32)
    up_grad = (hidden_grad * gate_pre * logistic).astype(jnp.bfloat16)
    gate_grad = (hidden_grad * up_pre * logistic * (1.0 + gate_pre * (1.0 - logistic))).astype(jnp.bfloat16)
    contract_rows = (((0,), (0,)), ((), ()))
    down_w_grad = lax.dot_general(hidden, grads, contract_rows, preferred_element_type=jnp.float32).astype(jnp.bfloat16)
    gate_w_grad = lax.dot_general(rows, gate_grad, contract_rows, preferred_element_type=jnp.float32).astype(jnp.bfloat16)
    up_w_grad = lax.dot_general(rows, up_grad, contract_rows, preferred_element_type=jnp.float32).astype(jnp.bfloat16)
    return gate_grad, up_grad, gate_w_grad, up_w_grad, down_w_grad


def row_grads(gate_grad, up_grad, gate_w, up_w):
    row_total = gate_grad.shape[0]
    block = FF // N_DP
    contract_hidden = (((1,), (1,)), ((), ()))

    def step(running, index):
        first = index * block
        gate_piece = lax.dynamic_slice_in_dim(gate_grad, first, block, 1)
        up_piece = lax.dynamic_slice_in_dim(up_grad, first, block, 1)
        gate_cols = lax.dynamic_slice_in_dim(gate_w, first, block, 1)
        up_cols = lax.dynamic_slice_in_dim(up_w, first, block, 1)
        partial_term = lax.dot_general(gate_piece, gate_cols, contract_hidden, preferred_element_type=jnp.float32)
        partial_term = partial_term + lax.dot_general(up_piece, up_cols, contract_hidden, preferred_element_type=jnp.float32)
        rounded = lax.optimization_barrier(partial_term.astype(jnp.bfloat16))
        return running + rounded.astype(jnp.float32), None

    running, _ = lax.scan(step, jnp.zeros((row_total, D), jnp.float32), jnp.arange(N_DP, dtype=jnp.int32))
    return running.astype(jnp.bfloat16)


def reference(tokens, grad_out, expert_ids, gate_codes, lengths, w_gate, w_up, w_down):
    experts = EXPERTS
    tok_blocks = tokens.reshape(DEVICES, TOK_DEV, D)
    grad_blocks = grad_out.reshape(DEVICES, TOK_DEV, D)
    id_blocks = expert_ids.reshape(DEVICES, TOK_DEV, TOPK)
    code_blocks = gate_codes.reshape(DEVICES, TOK_DEV, TOPK)

    def per_device(items):
        tok_block, grad_block, id_block, code_block, length_row = items
        select, slot_gate = slot_tables(id_block, code_block, length_row, experts)
        sent_tokens = jnp.einsum("ect,td->ecd", select, tok_block.astype(jnp.float32), precision=HIGHEST).astype(jnp.bfloat16)
        picked = jnp.einsum("ect,td->ecd", select, grad_block.astype(jnp.float32), precision=HIGHEST)
        sent_grads = (slot_gate[:, :, None] * picked).astype(jnp.bfloat16)
        return select, sent_tokens, sent_grads

    select, sent_tokens, sent_grads = lax.map(per_device, (tok_blocks, grad_blocks, id_blocks, code_blocks, lengths))
    expert_tokens = jnp.transpose(sent_tokens, (1, 0, 2, 3)).reshape(experts, DEVICES * CAP, D)
    expert_grads = jnp.transpose(sent_grads, (1, 0, 2, 3)).reshape(experts, DEVICES * CAP, D)

    def per_expert(items):
        rows, grads, gate_w, up_w, down_w = items
        gate_grad, up_grad, gate_w_grad, up_w_grad, down_w_grad = expert_pass(rows, grads, gate_w, up_w, down_w)
        slot_grad = row_grads(gate_grad, up_grad, gate_w, up_w)
        return slot_grad, gate_w_grad, up_w_grad, down_w_grad

    slot_grad, grad_gate_w, grad_up_w, grad_down_w = lax.map(per_expert, (expert_tokens, expert_grads, w_gate, w_up, w_down))
    returned = jnp.transpose(slot_grad.reshape(experts, DEVICES, CAP, D), (1, 0, 2, 3))
    combined = jnp.einsum("nect,necd->ntd", select, returned.astype(jnp.float32), precision=HIGHEST)
    grad_tokens = combined.astype(jnp.bfloat16).reshape(TOKENS, D)
    return grad_tokens, grad_gate_w, grad_up_w, grad_down_w
```

```python
import functools

import jax
import jax.numpy as jnp
from jax import lax
from jax.experimental import pallas as pl
from jax.experimental.pallas import tpu as pltpu
from jax.sharding import PartitionSpec as P

CAP = 6
CHUNK = 2
CHUNKS = CAP // CHUNK
PARTS = 4
GRID_SCALE = 2048.0
BF16 = jnp.bfloat16
F32 = jnp.float32
VMEM_LIMIT = 48 * 1024 * 1024


def dot(a, b, contract):
    return lax.dot_general(a, b, (contract, ((), ())), preferred_element_type=F32)


def select_kernel(
    lengths_ref, ids_ref, codes_ref, tok0_ref, tok1_ref, grad0_ref, grad1_ref,
    out0_ref, out1_ref, out2_ref, table_ref, scale_ref,
):
    experts, tok_count = ids_ref.shape[0], ids_ref.shape[1]
    row_count = experts * CHUNK * PARTS

    @pl.when(pl.program_id(0) == 0)
    def _():
        ids = ids_ref[...]
        codes = codes_ref[...]
        slot_len = tok_count // 2
        position = lax.broadcasted_iota(jnp.int32, (1, tok_count), 1)
        bound = jnp.where(
            position < slot_len, lengths_ref[0, 0], lengths_ref[0, 1] + slot_len
        )
        live = position < bound
        expert = lax.broadcasted_iota(jnp.int32, (experts, tok_count), 0)
        member = jnp.zeros((experts, tok_count), F32)
        gate = jnp.zeros((experts, tok_count), F32)
        for e in range(experts):
            hit = ids == e
            found = jnp.sum(hit.astype(F32), axis=0, keepdims=True)
            code = jnp.sum(jnp.where(hit, codes, 0).astype(F32), axis=0, keepdims=True)
            member = jnp.where(
                jnp.logical_and(expert == e, jnp.logical_and(live, found > 0.0)),
                1.0,
                member,
            )
            gate = jnp.where(expert == e, code / GRID_SCALE, gate)
        earlier = lax.broadcasted_iota(jnp.int32, (tok_count, tok_count), 0)
        later = lax.broadcasted_iota(jnp.int32, (tok_count, tok_count), 1)
        before = (earlier < later).astype(BF16)
        rank = dot(member.astype(BF16), before, ((1,), (0,)))
        slot_of = jnp.where(member > 0.0, rank, -1.0)

        def spread(x):
            return jnp.broadcast_to(
                x[:, None, :], (experts, row_count // experts, tok_count)
            ).reshape(row_count, tok_count)

        slot_rows = spread(slot_of)
        gate_rows = spread(gate)
        row = lax.broadcasted_iota(jnp.int32, (row_count, tok_count), 0)
        in_chunk = ((row // PARTS) % CHUNK).astype(F32)
        is_grad = ((row // 2) % 2)[:, :1] == 1
        for c in range(CHUNKS):
            chosen = slot_rows == in_chunk + float(c * CHUNK)
            table_ref[c] = chosen.astype(BF16)
            weight = jnp.sum(jnp.where(chosen, gate_rows, 0.0), axis=1, keepdims=True)
            scale_ref[c] = jnp.broadcast_to(
                jnp.where(is_grad, weight, 1.0), scale_ref.shape[1:]
            )

    row = lax.broadcasted_iota(jnp.int32, (row_count, tok_count), 0)
    pieces = (tok0_ref, tok1_ref, grad0_ref, grad1_ref)
    for c, out_ref in enumerate((out0_ref, out1_ref, out2_ref)):
        table = table_ref[c]
        total = None
        for part in range(PARTS):
            mine = jnp.where(row % PARTS == part, table, jnp.zeros_like(table))
            term = dot(mine, pieces[part][...], ((1,), (0,)))
            total = term if total is None else total + term
        out_ref[...] = (scale_ref[c][:, :1] * total).astype(BF16)


def select_rows(tokens, grad_out, expert_ids, gate_codes, lengths, experts):
    tok_count, width = tokens.shape
    half = width // 2
    tile = 512
    steps = half // tile
    row_count = experts * CHUNK * PARTS
    first = pl.BlockSpec((tok_count, tile), lambda j: (0, j))
    second = pl.BlockSpec((tok_count, tile), lambda j: (0, j + steps))
    whole = pl.BlockSpec((experts, tok_count), lambda j: (0, 0))
    block = pl.BlockSpec((row_count, tile), lambda j: (0, j))
    return pl.pallas_call(
        select_kernel,
        grid=(steps,),
        in_specs=[
            pl.BlockSpec(memory_space=pltpu.SMEM), whole, whole, first, second, first, second,
        ],
        out_specs=[block] * CHUNKS
        + [pl.BlockSpec((CHUNKS, row_count, tok_count), lambda j: (0, 0, 0))],
        out_shape=[jax.ShapeDtypeStruct((row_count, half), BF16)] * CHUNKS
        + [jax.ShapeDtypeStruct((CHUNKS, row_count, tok_count), BF16)],
        scratch_shapes=[pltpu.VMEM((CHUNKS, row_count, 128), F32)],
        compiler_params=pltpu.CompilerParams(vmem_limit_bytes=VMEM_LIMIT),
        name="select_rows",
    )(lengths, expert_ids.T, gate_codes.T, tokens, tokens, grad_out, grad_out)


def unfold_kernel(x_ref, out_ref):
    rows, folded = out_ref.shape[0], x_ref.shape[0]
    to = lax.broadcasted_iota(jnp.int32, (rows, folded), 0)
    src = lax.broadcasted_iota(jnp.int32, (rows, folded), 1)
    pick = (src == to * PARTS + pl.program_id(0)).astype(BF16)
    out_ref[...] = dot(pick, x_ref[...], ((1,), (0,))).astype(BF16)


def unfold(x):
    folded, width = x.shape
    rows = folded // PARTS
    return pl.pallas_call(
        unfold_kernel,
        grid=(PARTS,),
        in_specs=[pl.BlockSpec((folded, width), lambda p: (0, 0))],
        out_specs=pl.BlockSpec((rows, width), lambda p: (0, p)),
        out_shape=jax.ShapeDtypeStruct((rows, width * PARTS), BF16),
        compiler_params=pltpu.CompilerParams(vmem_limit_bytes=VMEM_LIMIT),
        name="unfold",
    )(x)


def fold_kernel(x_ref, out_ref):
    rows, folded = x_ref.shape[0], out_ref.shape[0]
    width = out_ref.shape[1]
    to = lax.broadcasted_iota(jnp.int32, (folded, rows), 0)
    src = lax.broadcasted_iota(jnp.int32, (folded, rows), 1)
    total = None
    for part in range(PARTS):
        place = (to == src * PARTS + part).astype(BF16)
        term = dot(place, x_ref[:, part * width : (part + 1) * width], ((1,), (0,)))
        total = term if total is None else total + term
    out_ref[...] = total.astype(BF16)


def fold(x):
    rows, width = x.shape
    return pl.pallas_call(
        fold_kernel,
        out_shape=jax.ShapeDtypeStruct((rows * PARTS, width // PARTS), BF16),
        compiler_params=pltpu.CompilerParams(vmem_limit_bytes=VMEM_LIMIT),
        name="fold",
    )(x)


def chunk_kernel(rows_ref, grads_ref, gate_w_ref, up_w_ref, down_w_ref,
                 hidden_ref, both_ref, term_ref, gate_acc, up_acc, hid_acc):
    step = pl.program_id(0)
    tiles = pl.num_programs(0) // 2
    tile = rows_ref.shape[1]

    @pl.when(step == 0)
    def _():
        gate_acc[...] = jnp.zeros_like(gate_acc)
        up_acc[...] = jnp.zeros_like(up_acc)
        hid_acc[...] = jnp.zeros_like(hid_acc)

    @pl.when(step < tiles)
    def _():
        span = pl.ds(pl.multiple_of(step * tile, tile), tile)
        rows = rows_ref[...]
        gate_acc[...] += dot(rows, gate_w_ref[span, :], ((1,), (0,)))
        up_acc[...] += dot(rows, up_w_ref[span, :], ((1,), (0,)))
        hid_acc[...] += dot(grads_ref[...], down_w_ref[...], ((1,), (1,)))

    @pl.when(step == tiles - 1)
    def _():
        gate_pre, up_pre, hidden_grad = gate_acc[...], up_acc[...], hid_acc[...]
        logistic = 1.0 / (1.0 + jnp.exp(-gate_pre))
        hidden_ref[...] = (gate_pre * logistic * up_pre).astype(BF16)
        units = gate_pre.shape[1]
        both_ref[:, :units] = (
            hidden_grad * up_pre * logistic * (1.0 + gate_pre * (1.0 - logistic))
        ).astype(BF16)
        both_ref[:, units:] = (hidden_grad * gate_pre * logistic).astype(BF16)

    @pl.when(step >= tiles)
    def _():
        span = pl.ds(pl.multiple_of((step - tiles) * tile, tile), tile)
        units = gate_acc.shape[1]
        term = dot(both_ref[:, :units], gate_w_ref[span, :], ((1,), (1,)))
        term += dot(both_ref[:, units:], up_w_ref[span, :], ((1,), (1,)))
        term_ref[...] = term.astype(BF16)


def chunk_pass(gathered, gate_w, up_w, down_w):
    row_count = gathered.shape[0]
    width, units = gate_w.shape
    tile = 1024
    tiles = width // tile
    last = tiles - 1
    return pl.pallas_call(
        chunk_kernel,
        grid=(2 * tiles,),
        in_specs=[
            pl.BlockSpec((row_count, tile), lambda j: (0, jnp.minimum(j, last))),
            pl.BlockSpec((row_count, tile), lambda j: (0, jnp.minimum(j, last) + tiles)),
            pl.BlockSpec((width, units), lambda j: (0, 0)),
            pl.BlockSpec((width, units), lambda j: (0, 0)),
            pl.BlockSpec((units, tile), lambda j: (0, jnp.minimum(j, last))),
        ],
        out_specs=[
            pl.BlockSpec((row_count, units), lambda j: (0, 0)),
            pl.BlockSpec((row_count, 2 * units), lambda j: (0, 0)),
            pl.BlockSpec((row_count, tile), lambda j: (0, jnp.maximum(j - tiles, 0))),
        ],
        out_shape=[
            jax.ShapeDtypeStruct((row_count, units), BF16),
            jax.ShapeDtypeStruct((row_count, 2 * units), BF16),
            jax.ShapeDtypeStruct((row_count, width), BF16),
        ],
        scratch_shapes=[pltpu.VMEM((row_count, units), F32)] * 3,
        compiler_params=pltpu.CompilerParams(vmem_limit_bytes=VMEM_LIMIT),
        cost_estimate=pl.CostEstimate(
            flops=2 * 5 * row_count * width * units,
            bytes_accessed=2 * (3 * row_count * width + 3 * width * units),
            transcendentals=row_count * units,
        ),
        name="chunk_pass",
    )(gathered, gathered, gate_w, up_w, down_w)


def weight_kernel(*refs):
    rows_refs, grads_refs = refs[:CHUNKS], refs[CHUNKS : 2 * CHUNKS]
    hidden_refs, both_refs = refs[2 * CHUNKS : 3 * CHUNKS], refs[3 * CHUNKS : 4 * CHUNKS]
    gate_ref, up_ref, down_ref = refs[4 * CHUNKS :]
    units = gate_ref.shape[1]
    inner, outer = None, None
    for c in range(CHUNKS):
        term = dot(rows_refs[c][...], both_refs[c][...], ((0,), (0,)))
        inner = term if inner is None else inner + term
        term = dot(hidden_refs[c][...], grads_refs[c][...], ((0,), (0,)))
        outer = term if outer is None else outer + term
    gate_ref[...] = inner[:, :units].astype(BF16)
    up_ref[...] = inner[:, units:].astype(BF16)
    down_ref[...] = outer.astype(BF16)


def weight_grads(gathered, hidden, both):
    row_count = gathered[0].shape[0]
    width = gathered[0].shape[1] // 2
    units = hidden[0].shape[1]
    tile = 512
    tiles = width // tile
    return pl.pallas_call(
        weight_kernel,
        grid=(tiles,),
        in_specs=[pl.BlockSpec((row_count, tile), lambda j: (0, j))] * CHUNKS
        + [pl.BlockSpec((row_count, tile), lambda j: (0, j + tiles))] * CHUNKS
        + [pl.BlockSpec((row_count, units), lambda j: (0, 0))] * CHUNKS
        + [pl.BlockSpec((row_count, 2 * units), lambda j: (0, 0))] * CHUNKS,
        out_specs=[
            pl.BlockSpec((tile, units), lambda j: (j, 0)),
            pl.BlockSpec((tile, units), lambda j: (j, 0)),
            pl.BlockSpec((units, tile), lambda j: (0, j)),
        ],
        out_shape=[
            jax.ShapeDtypeStruct((width, units), BF16),
            jax.ShapeDtypeStruct((width, units), BF16),
            jax.ShapeDtypeStruct((units, width), BF16),
        ],
        compiler_params=pltpu.CompilerParams(vmem_limit_bytes=VMEM_LIMIT),
        cost_estimate=pl.CostEstimate(
            flops=2 * 3 * CHUNKS * row_count * width * units,
            bytes_accessed=2 * (2 * CHUNKS * row_count * width + 3 * width * units),
            transcendentals=0,
        ),
        name="weight_grads",
    )(*gathered, *gathered, *hidden, *both)


def combine_kernel(table_ref, *refs):
    part_refs, out_ref = refs[:-1], refs[-1]
    part = pl.program_id(0)
    total = None
    for c, part_ref in enumerate(part_refs):
        table = table_ref[c]
        row = lax.broadcasted_iota(jnp.int32, table.shape, 0)
        mine = jnp.where(row % PARTS == part, table, jnp.zeros_like(table))
        term = dot(mine, part_ref[...], ((0,), (0,)))
        total = term if total is None else total + term
    out_ref[...] = total.astype(BF16)


def combine(table, parts):
    folded, width = parts[0].shape
    tok_count = table.shape[2]
    return pl.pallas_call(
        combine_kernel,
        grid=(PARTS,),
        in_specs=[pl.BlockSpec(table.shape, lambda p: (0, 0, 0))]
        + [pl.BlockSpec((folded, width), lambda p: (0, 0))] * CHUNKS,
        out_specs=pl.BlockSpec((tok_count, width), lambda p: (0, p)),
        out_shape=jax.ShapeDtypeStruct((tok_count, width * PARTS), BF16),
        compiler_params=pltpu.CompilerParams(vmem_limit_bytes=VMEM_LIMIT),
        name="combine",
    )(table, *parts)


def exchange(x, experts):
    folded, width = x.shape
    blocks = x.reshape(experts, folded // experts, width)
    return lax.all_to_all(
        blocks, ("grp", "sp"), split_axis=0, concat_axis=0, tiled=True
    ).reshape(folded, width)


def body(tokens, grad_out, expert_ids, gate_codes, lengths, w_gate, w_up, w_down):
    experts = lax.axis_size("grp") * lax.axis_size("sp")
    *sent, table = select_rows(tokens, grad_out, expert_ids, gate_codes, lengths, experts)
    gate_w, up_w, down_w = w_gate[0], w_up[0], w_down[0]
    gathered, hidden, both, parts = [], [], [], []
    for c in range(CHUNKS):
        arrived = unfold(exchange(sent[c], experts))
        gathered.append(lax.all_gather(arrived, "dp", axis=0, tiled=True))
    for c in range(CHUNKS):
        hidden_c, both_c, term = chunk_pass(gathered[c], gate_w, up_w, down_w)
        hidden.append(hidden_c)
        both.append(both_c)
        summed = lax.psum_scatter(term, "dp", scatter_dimension=0, tiled=True)
        parts.append(exchange(fold(summed), experts))
    gate_w_grad, up_w_grad, down_w_grad = weight_grads(gathered, hidden, both)
    grad_tokens = combine(table, parts)
    return (grad_tokens, gate_w_grad[None], up_w_grad[None], down_w_grad[None])


def solution(mesh):
    return jax.shard_map(
        body,
        mesh=mesh,
        in_specs=(
            P(("grp", "dp", "sp"), None),
            P(("grp", "dp", "sp"), None),
            P(("grp", "dp", "sp"), None),
            P(("grp", "dp", "sp"), None),
            P(("grp", "dp", "sp"), None),
            P(("grp", "sp"), None, "dp"),
            P(("grp", "sp"), None, "dp"),
            P(("grp", "sp"), "dp", None),
        ),
        out_specs=(
            P(("grp", "dp", "sp"), None),
            P(("grp", "sp"), None, "dp"),
            P(("grp", "sp"), None, "dp"),
            P(("grp", "sp"), "dp", None),
        ),
        check_vma=False,
    )
```

```python
import jax
import jax.numpy as jnp
from jax import lax
from jax.experimental import pallas as pl
from jax.experimental.pallas import tpu as pltpu
from jax.sharding import PartitionSpec as P

CAP = 6
SIDE = 4
GRID_SCALE = 2048.0
BF16 = jnp.bfloat16
F32 = jnp.float32
PARAMS = pltpu.CompilerParams(vmem_limit_bytes=48 * 1024 * 1024)
SMEM = pl.BlockSpec(memory_space=pltpu.SMEM)
VMEM = pl.BlockSpec(memory_space=pltpu.VMEM)


def dot(a, b, contract):
    return lax.dot_general(a, b, (contract, ((), ())), preferred_element_type=F32)


NN = ((1,), (0,))
NT = ((1,), (1,))
TN = ((0,), (0,))


def shape(*dims, dtype=BF16):
    return jax.ShapeDtypeStruct(dims, dtype)


def shift(x, along_a, step):
    pairs = []
    for grp in range(2):
        for y in range(SIDE):
            for z in range(SIDE):
                if (grp == 0) == along_a:
                    to = (y, (z + step) % SIDE)
                else:
                    to = ((y + step) % SIDE, z)
                pairs.append(
                    (grp * SIDE * SIDE + y * SIDE + z, grp * SIDE * SIDE + to[0] * SIDE + to[1])
                )
    return lax.ppermute(x, ("grp", "dp"), pairs)


def pack_kernel(quarter_ref, gate_ref, up_ref, down_ref, out_ref):
    units = gate_ref.shape[1]
    out_ref[:, :units] = gate_ref[...]
    out_ref[:, units : 2 * units] = up_ref[...]
    out_ref[:, 2 * units :] = down_ref[...].T


def pack_weights(quarter, gate_w, up_w, down_w):
    width, units = gate_w.shape
    part = width // SIDE
    tile = part // 2
    return pl.pallas_call(
        pack_kernel,
        grid_spec=pltpu.PrefetchScalarGridSpec(
            num_scalar_prefetch=1,
            grid=(2,),
            in_specs=[
                pl.BlockSpec((tile, units), lambda j, q: (q[0] * 2 + j, 0)),
                pl.BlockSpec((tile, units), lambda j, q: (q[0] * 2 + j, 0)),
                pl.BlockSpec((units, tile), lambda j, q: (0, q[0] * 2 + j)),
            ],
            out_specs=pl.BlockSpec((tile, 3 * units), lambda j, q: (j, 0)),
        ),
        out_shape=shape(part, 3 * units),
        compiler_params=PARAMS,
        name="pack_weights",
    )(quarter, gate_w, up_w, down_w)


def select_kernel(lengths_ref, ids_ref, codes_ref, *refs):
    pieces, (out_ref, table_ref, rows_ref, scale_ref) = refs[: 2 * SIDE], refs[2 * SIDE :]
    experts, tok_count = ids_ref.shape
    folded = 2 * SIDE * CAP
    row_count = experts * folded

    @pl.when(pl.program_id(0) == 0)
    def _():
        ids = ids_ref[...]
        codes = codes_ref[...]
        slot_len = tok_count // 2
        position = lax.broadcasted_iota(jnp.int32, (1, tok_count), 1)
        bound = jnp.where(
            position < slot_len, lengths_ref[0, 0], lengths_ref[0, 1] + slot_len
        )
        live = position < bound
        expert = lax.broadcasted_iota(jnp.int32, (experts, tok_count), 0)
        member = jnp.zeros((experts, tok_count), F32)
        gate = jnp.zeros((experts, tok_count), F32)
        for e in range(experts):
            hit = ids == e
            found = jnp.sum(hit.astype(F32), axis=0, keepdims=True)
            code = jnp.sum(jnp.where(hit, codes, 0).astype(F32), axis=0, keepdims=True)
            member = jnp.where(
                jnp.logical_and(expert == e, jnp.logical_and(live, found > 0.0)),
                1.0,
                member,
            )
            gate = jnp.where(expert == e, code / GRID_SCALE, gate)
        earlier = lax.broadcasted_iota(jnp.int32, (tok_count, tok_count), 0)
        later = lax.broadcasted_iota(jnp.int32, (tok_count, tok_count), 1)
        rank = dot(member.astype(BF16), (earlier < later).astype(BF16), NN)
        slot_of = jnp.where(member > 0.0, rank, -1.0)

        def spread(x, times):
            return jnp.broadcast_to(
                x[:, None, :], (experts, times, tok_count)
            ).reshape(experts * times, tok_count)

        row = lax.broadcasted_iota(jnp.int32, (row_count, tok_count), 0)
        chosen = spread(slot_of, folded) == (row % CAP).astype(F32)
        rows_ref[...] = chosen.astype(BF16)
        weight = jnp.sum(
            jnp.where(chosen, spread(gate, folded), 0.0), axis=1, keepdims=True
        )
        is_grad = ((row // CAP) % 2)[:, :1] == 1
        scale_ref[...] = jnp.broadcast_to(jnp.where(is_grad, weight, 1.0), scale_ref.shape)
        row = lax.broadcasted_iota(jnp.int32, table_ref.shape, 0)
        table_ref[...] = (
            spread(slot_of, SIDE * CAP) == (row % CAP).astype(F32)
        ).astype(BF16)

    row = lax.broadcasted_iota(jnp.int32, (row_count, tok_count), 0)
    chosen = rows_ref[...]
    total = None
    for p in range(2 * SIDE):
        mine = jnp.where((row // CAP) % (2 * SIDE) == p, chosen, jnp.zeros_like(chosen))
        term = dot(mine, pieces[p][...], NN)
        total = term if total is None else total + term
    out_ref[...] = (scale_ref[:, :1] * total).astype(BF16)


def select_rows(tokens, grad_out, expert_ids, gate_codes, lengths, experts):
    tok_count, width = tokens.shape
    part = width // SIDE
    steps = 2
    tile = part // steps
    row_count = experts * 2 * SIDE * CAP
    table_rows = experts * SIDE * CAP
    whole = pl.BlockSpec((experts, tok_count), lambda j: (0, 0))
    pieces, piece_specs = [], []
    for q in range(SIDE):
        for array in (tokens, grad_out):
            pieces.append(array)
            piece_specs.append(
                pl.BlockSpec((tok_count, tile), lambda j, q=q: (0, q * steps + j))
            )
    return pl.pallas_call(
        select_kernel,
        grid=(steps,),
        in_specs=[SMEM, whole, whole] + piece_specs,
        out_specs=[
            pl.BlockSpec((row_count, tile), lambda j: (0, j)),
            pl.BlockSpec((table_rows, tok_count), lambda j: (0, 0)),
        ],
        out_shape=[shape(row_count, part), shape(table_rows, tok_count)],
        scratch_shapes=[
            pltpu.VMEM((row_count, tok_count), BF16),
            pltpu.VMEM((row_count, 128), F32),
        ],
        compiler_params=PARAMS,
        name="select_rows",
    )(lengths, expert_ids.T, gate_codes.T, *pieces)


def exchange(x, experts):
    folded, width = x.shape
    blocks = x.reshape(experts, folded // experts, width)
    return lax.all_to_all(
        blocks, ("grp", "sp"), split_axis=0, concat_axis=0, tiled=True
    ).reshape(folded, width)


def unfold_kernel(a_ref, x_ref, *out_refs):
    rows, folded = out_refs[0].shape[0], x_ref.shape[0]
    part = x_ref.shape[1]
    to = lax.broadcasted_iota(jnp.int32, (rows, folded), 0)
    src = lax.broadcasted_iota(jnp.int32, (rows, folded), 1)
    first = (to // CAP) * (2 * SIDE * CAP) + to % CAP
    for d, out_ref in enumerate(out_refs):
        quarter = (a_ref[0] + d) % SIDE
        for array in range(2):
            pick = (src == first + (quarter * 2 + array) * CAP).astype(BF16)
            out_ref[:, array * part : (array + 1) * part] = dot(
                pick, x_ref[...], NN
            ).astype(BF16)


def unfold(a, x):
    folded, part = x.shape
    rows = folded // (2 * SIDE)
    return pl.pallas_call(
        unfold_kernel,
        in_specs=[SMEM, VMEM],
        out_shape=[shape(rows, 2 * part)] * SIDE,
        compiler_params=PARAMS,
        name="unfold",
    )(a, x)


def line_kernel(a_ref, *refs):
    out_ref = refs[-1]
    for d, x_ref in enumerate(refs[:-1]):
        rows = x_ref.shape[0]
        at = ((a_ref[0] + SIDE - d) % SIDE) * rows
        out_ref[pl.ds(pl.multiple_of(at, 16), rows), :] = x_ref[...]


def line_up(a, blocks):
    rows, width = blocks[0].shape
    return pl.pallas_call(
        line_kernel,
        in_specs=[SMEM] + [VMEM] * SIDE,
        out_shape=shape(SIDE * rows, width),
        compiler_params=PARAMS,
        name="line_up",
    )(a, *blocks)


def forward_kernel(*refs):
    pieces, weights, outs = refs[:-2 * SIDE], refs[-2 * SIDE : -SIDE], refs[-SIDE:]
    part = weights[0].shape[0]
    units = weights[0].shape[1] // 3
    rows = pieces[0].shape[0]
    for i, piece in enumerate(pieces):
        span = slice(i * rows, (i + 1) * rows)
        for weight, out in zip(weights, outs):
            inner = dot(piece[:, :part], weight[:, : 2 * units], NN)
            out[span, : 2 * units] = inner.astype(out.dtype)
            outer = dot(piece[:, part:], weight[:, 2 * units :], NN)
            out[span, 2 * units :] = outer.astype(out.dtype)


def forward(pieces, weights):
    rows = pieces[0].shape[0] * len(pieces)
    part, columns = weights[0].shape
    return pl.pallas_call(
        forward_kernel,
        in_specs=[VMEM] * (len(pieces) + SIDE),
        out_shape=[shape(rows, columns, dtype=F32)] + [shape(rows, columns)] * (SIDE - 1),
        compiler_params=PARAMS,
        cost_estimate=pl.CostEstimate(
            flops=2 * SIDE * rows * part * columns,
            bytes_accessed=4 * rows * part + 2 * SIDE * (part + rows) * columns,
            transcendentals=0,
        ),
        name="forward",
    )(*pieces, *weights)


def activate_kernel(*refs):
    terms, out_ref = refs[:-1], refs[-1]
    total = terms[0][...]
    for term in terms[1:]:
        total = total + term[...].astype(F32)
    units = total.shape[1] // 3
    gate_pre, up_pre, hidden_grad = (
        total[:, :units], total[:, units : 2 * units], total[:, 2 * units :],
    )
    logistic = 1.0 / (1.0 + jnp.exp(-gate_pre))
    out_ref[:, :units] = (gate_pre * logistic * up_pre).astype(BF16)
    out_ref[:, units : 2 * units] = (
        hidden_grad * up_pre * logistic * (1.0 + gate_pre * (1.0 - logistic))
    ).astype(BF16)
    out_ref[:, 2 * units :] = (hidden_grad * gate_pre * logistic).astype(BF16)


def activate(terms):
    return pl.pallas_call(
        activate_kernel,
        in_specs=[VMEM] * SIDE,
        out_shape=shape(*terms[0].shape),
        compiler_params=PARAMS,
        name="activate",
    )(*terms)


def backward_kernel(*refs):
    hidden, weights, outs = refs[:SIDE], refs[SIDE : 2 * SIDE], refs[2 * SIDE :]
    rows = outs[0].shape[0]
    units = hidden[0].shape[1] // 3
    for i, out in enumerate(outs):
        span = slice(i * rows, (i + 1) * rows)
        total = None
        for h, weight in zip(hidden, weights):
            term = dot(h[span, units:], weight[:, : 2 * units], NT)
            total = term if total is None else total + term
        out[...] = total.astype(out.dtype)


def backward(hidden, weights, dtypes):
    rows = hidden[0].shape[0] // len(dtypes)
    part, columns = weights[0].shape
    return pl.pallas_call(
        backward_kernel,
        in_specs=[VMEM] * (2 * SIDE),
        out_shape=[shape(rows, part, dtype=dtype) for dtype in dtypes],
        compiler_params=PARAMS,
        cost_estimate=pl.CostEstimate(
            flops=2 * SIDE * rows * len(dtypes) * part * columns * 2 // 3,
            bytes_accessed=2 * SIDE * (part + rows * len(dtypes)) * columns,
            transcendentals=0,
        ),
        name="backward",
    )(*hidden, *weights)


def weight_kernel(*refs):
    pieces, hidden, out_ref = refs[:SIDE], refs[SIDE:-1], refs[-1]
    part = out_ref.shape[0]
    units = out_ref.shape[1] // 3
    rows = pieces[0].shape[0]
    inner, outer, i = None, None, 0
    for h in hidden:
        for k in range(h.shape[0] // rows):
            span = slice(k * rows, (k + 1) * rows)
            piece = pieces[i]
            term = dot(piece[:, :part], h[span, units:], TN)
            inner = term if inner is None else inner + term
            term = dot(piece[:, part:], h[span, :units], TN)
            outer = term if outer is None else outer + term
            i += 1
    out_ref[:, : 2 * units] = inner.astype(BF16)
    out_ref[:, 2 * units :] = outer.astype(BF16)


def weight_grads(pieces, hidden):
    part = pieces[0].shape[1] // 2
    columns = hidden[0].shape[1]
    rows = pieces[0].shape[0] * SIDE
    return pl.pallas_call(
        weight_kernel,
        in_specs=[VMEM] * (SIDE + len(hidden)),
        out_shape=shape(part, columns),
        compiler_params=PARAMS,
        cost_estimate=pl.CostEstimate(
            flops=2 * rows * part * columns,
            bytes_accessed=4 * rows * part + 2 * (part + rows) * columns,
            transcendentals=0,
        ),
        name="weight_grads",
    )(*pieces, *hidden)


def unpack_kernel(quarter_ref, x_ref, *refs):
    gate_ref, up_ref, down_ref = refs[-3:]
    units = gate_ref.shape[1]
    gate_ref[...] = x_ref[:, :units]
    up_ref[...] = x_ref[:, units : 2 * units]
    down_ref[...] = x_ref[:, 2 * units :].T


def unpack(quarter, x, into):
    part, columns = x.shape
    units, width = columns // 3, part * SIDE
    tile = part // 2
    earlier = [] if into is None else list(into)
    return pl.pallas_call(
        unpack_kernel,
        grid_spec=pltpu.PrefetchScalarGridSpec(
            num_scalar_prefetch=1,
            grid=(2,),
            in_specs=[pl.BlockSpec((tile, columns), lambda j, q: (j, 0))]
            + [pl.BlockSpec(memory_space=pl.ANY)] * len(earlier),
            out_specs=[
                pl.BlockSpec((tile, units), lambda j, q: (q[0] * 2 + j, 0)),
                pl.BlockSpec((tile, units), lambda j, q: (q[0] * 2 + j, 0)),
                pl.BlockSpec((units, tile), lambda j, q: (0, q[0] * 2 + j)),
            ],
        ),
        out_shape=[shape(width, units), shape(width, units), shape(units, width)],
        input_output_aliases={2 + i: i for i in range(len(earlier))},
        compiler_params=PARAMS,
        name="unpack",
    )(quarter, x, *earlier)


def sum_kernel(a_ref, *refs):
    terms, outs = refs[:SIDE], refs[SIDE:]
    rows = outs[0].shape[0]
    for d, out in enumerate(outs):
        at = pl.multiple_of(((a_ref[0] + d) % SIDE) * rows, 16)
        total = None
        for term in terms:
            x = term[pl.ds(at, rows), :].astype(F32)
            total = x if total is None else total + x
        out[...] = total.astype(BF16)


def sum_rows(a, terms):
    rows, part = terms[0].shape
    return pl.pallas_call(
        sum_kernel,
        in_specs=[SMEM] + [VMEM] * SIDE,
        out_shape=[shape(rows // SIDE, part)] * SIDE,
        compiler_params=PARAMS,
        name="sum_rows",
    )(a, *terms)


def fold_kernel(a_ref, *refs):
    out_ref = refs[-1]
    folded, rows = out_ref.shape[0], refs[0].shape[0]
    to = lax.broadcasted_iota(jnp.int32, (folded, rows), 0)
    src = lax.broadcasted_iota(jnp.int32, (folded, rows), 1)
    first = (src // CAP) * (SIDE * CAP) + src % CAP
    total = None
    for d, x_ref in enumerate(refs[:-1]):
        quarter = (a_ref[0] + SIDE - d) % SIDE
        term = dot((to == first + quarter * CAP).astype(BF16), x_ref[...], NN)
        total = term if total is None else total + term
    out_ref[...] = total.astype(BF16)


def fold(a, blocks):
    rows, part = blocks[0].shape
    return pl.pallas_call(
        fold_kernel,
        in_specs=[SMEM] + [VMEM] * SIDE,
        out_shape=shape(rows * SIDE, part),
        compiler_params=PARAMS,
        name="fold",
    )(a, *blocks)


def combine_kernel(table_ref, x_ref, out_ref):
    table = table_ref[...]
    row = lax.broadcasted_iota(jnp.int32, table.shape, 0)
    quarter = pl.program_id(0)
    mine = jnp.where((row // CAP) % SIDE == quarter, table, jnp.zeros_like(table))
    out_ref[...] = dot(mine, x_ref[...], TN).astype(BF16)


def combine(table, x):
    folded, part = x.shape
    tok_count = table.shape[1]
    return pl.pallas_call(
        combine_kernel,
        grid=(SIDE,),
        in_specs=[
            pl.BlockSpec(table.shape, lambda q: (0, 0)),
            pl.BlockSpec((folded, part), lambda q: (0, 0)),
        ],
        out_specs=pl.BlockSpec((tok_count, part), lambda q: (0, q)),
        out_shape=shape(tok_count, part * SIDE),
        compiler_params=PARAMS,
        name="combine",
    )(table, x)


def body(tokens, grad_out, expert_ids, gate_codes, lengths, w_gate, w_up, w_down):
    experts = lax.axis_size("grp") * lax.axis_size("sp")
    dp = lax.axis_index("dp")
    a = jnp.where(lax.axis_index("grp") == 0, dp % SIDE, dp // SIDE).astype(jnp.int32)[None]
    quarters = [(a + d) % SIDE for d in range(SIDE)]
    gate_w, up_w, down_w = w_gate[0], w_up[0], w_down[0]

    weights = [pack_weights(quarters[d], gate_w, up_w, down_w) for d in range(SIDE)]
    weights = [weights[0]] + [shift(weights[d], True, d) for d in range(1, SIDE)]

    sent, table = select_rows(tokens, grad_out, expert_ids, gate_codes, lengths, experts)
    blocks = unfold(a, exchange(sent, experts))
    blocks = [blocks[0]] + [shift(blocks[d], True, d) for d in range(1, SIDE)]
    line = line_up(a, blocks)
    steps = (0, 1, -1, 2)
    pieces = [line] + [shift(line, False, step) for step in steps[1:]]

    terms = forward(pieces, weights)
    terms = [terms[0]] + [shift(terms[d], True, -d) for d in range(1, SIDE)]
    acts = activate(terms)
    hidden = [acts] + [shift(acts, True, d) for d in range(1, SIDE)]

    row_terms = backward(hidden, weights, [F32, BF16, BF16, BF16])
    row_terms = [row_terms[0]] + [
        shift(row_terms[i], False, -steps[i]) for i in range(1, SIDE)
    ]
    parts = sum_rows(a, row_terms)
    parts = [parts[0]] + [shift(parts[d], True, d) for d in range(1, SIDE)]
    grad_tokens = combine(table, exchange(fold(a, parts), experts))

    order = (1, 3, 2, 0)
    grads = {d: weight_grads(pieces, [hidden[d]]) for d in order}
    grads = {d: shift(grads[d], True, -d) if d else grads[d] for d in order}
    into = None
    for d in (0, 1, 3, 2):
        into = unpack(quarters[d], grads[d], into)
    gate_w_grad, up_w_grad, down_w_grad = into
    return (grad_tokens, gate_w_grad[None], up_w_grad[None], down_w_grad[None])


def solution(mesh):
    return jax.shard_map(
        body,
        mesh=mesh,
        in_specs=(
            P(("grp", "dp", "sp"), None),
            P(("grp", "dp", "sp"), None),
            P(("grp", "dp", "sp"), None),
            P(("grp", "dp", "sp"), None),
            P(("grp", "dp", "sp"), None),
            P(("grp", "sp"), None, "dp"),
            P(("grp", "sp"), None, "dp"),
            P(("grp", "sp"), "dp", None),
        ),
        out_specs=(
            P(("grp", "dp", "sp"), None),
            P(("grp", "sp"), None, "dp"),
            P(("grp", "sp"), None, "dp"),
            P(("grp", "sp"), "dp", None),
        ),
        check_vma=False,
    )
```

```python
import functools

import jax
import jax.numpy as jnp
from jax import lax
from jax.experimental import pallas as pl
from jax.experimental.pallas import tpu as pltpu
from jax.sharding import PartitionSpec as P

CAP = 6
SIDE = 4
GRID_SCALE = 2048.0
BF16 = jnp.bfloat16
F32 = jnp.float32
MIB = 1024 * 1024
PARAMS = pltpu.CompilerParams(vmem_limit_bytes=24 * MIB)
SMEM = pl.BlockSpec(memory_space=pltpu.SMEM)
VMEM = pl.BlockSpec(memory_space=pltpu.VMEM)
ANY = pl.BlockSpec(memory_space=pl.ANY)


def dot(a, b, contract):
    return lax.dot_general(a, b, (contract, ((), ())), preferred_element_type=F32)


NN = ((1,), (0,))
NT = ((1,), (1,))
TN = ((0,), (0,))


def shape(*dims, dtype=BF16):
    return jax.ShapeDtypeStruct(dims, dtype)


def shift(x, along_a, step):
    pairs = []
    for grp in range(2):
        for y in range(SIDE):
            for z in range(SIDE):
                if (grp == 0) == along_a:
                    to = (y, (z + step) % SIDE)
                else:
                    to = ((y + step) % SIDE, z)
                pairs.append(
                    (grp * SIDE * SIDE + y * SIDE + z, grp * SIDE * SIDE + to[0] * SIDE + to[1])
                )
    return lax.ppermute(x, ("grp", "dp"), pairs)


def pack_kernel(a_ref, gate_ref, up_ref, down_ref, *out_refs):
    units = gate_ref.shape[1]
    part = out_refs[0].shape[0]
    for d, out_ref in enumerate(out_refs):
        at = pl.multiple_of(((a_ref[0] + d) % SIDE) * part, 128)
        span = pl.ds(at, part)
        out_ref[:, :units] = gate_ref[span, :]
        out_ref[:, units : 2 * units] = up_ref[span, :]
        out_ref[:, 2 * units :] = down_ref[:, span].T


def pack_weights(a, gate_w, up_w, down_w):
    width, units = gate_w.shape
    return pl.pallas_call(
        pack_kernel,
        in_specs=[SMEM, VMEM, VMEM, VMEM],
        out_shape=[shape(width // SIDE, 3 * units)] * SIDE,
        compiler_params=PARAMS,
        name="pack_weights",
    )(a, gate_w, up_w, down_w)


def table_kernel(lengths_ref, ids_ref, codes_ref, rows_ref, scale_ref, table_ref):
    experts, tok_count = ids_ref.shape
    folded = 2 * SIDE * CAP
    row_count = experts * folded
    ids = ids_ref[...]
    codes = codes_ref[...]
    slot_len = tok_count // 2
    position = lax.broadcasted_iota(jnp.int32, (1, tok_count), 1)
    bound = jnp.where(position < slot_len, lengths_ref[0, 0], lengths_ref[0, 1] + slot_len)
    live = position < bound
    expert = lax.broadcasted_iota(jnp.int32, (experts, tok_count), 0)
    member = jnp.zeros((experts, tok_count), F32)
    gate = jnp.zeros((experts, tok_count), F32)
    for e in range(experts):
        hit = ids == e
        found = jnp.sum(hit.astype(F32), axis=0, keepdims=True)
        code = jnp.sum(jnp.where(hit, codes, 0).astype(F32), axis=0, keepdims=True)
        here = jnp.logical_and(live, found > 0.0)
        member = jnp.where(jnp.logical_and(expert == e, here), 1.0, member)
        gate = jnp.where(expert == e, code / GRID_SCALE, gate)
    earlier = lax.broadcasted_iota(jnp.int32, (tok_count, tok_count), 0)
    later = lax.broadcasted_iota(jnp.int32, (tok_count, tok_count), 1)
    rank = dot(member.astype(BF16), (earlier < later).astype(BF16), NN)
    slot_of = jnp.where(member > 0.0, rank, -1.0)

    def spread(x, times):
        return jnp.broadcast_to(x[:, None, :], (experts, times, tok_count)).reshape(
            experts * times, tok_count
        )

    row = lax.broadcasted_iota(jnp.int32, (row_count, tok_count), 0)
    chosen = spread(slot_of, folded) == (row % CAP).astype(F32)
    part = (row // CAP) % (2 * SIDE)
    for p in range(2 * SIDE):
        mine = jnp.logical_and(chosen, part == p)
        rows_ref[:, p * tok_count : (p + 1) * tok_count] = mine.astype(BF16)
    weight = jnp.sum(jnp.where(chosen, spread(gate, folded), 0.0), axis=1, keepdims=True)
    is_grad = (part % 2)[:, :1] == 1
    scale_ref[...] = jnp.broadcast_to(jnp.where(is_grad, weight, 1.0), scale_ref.shape)
    row = lax.broadcasted_iota(jnp.int32, table_ref.shape, 0)
    chosen = spread(slot_of, SIDE * CAP) == (row % CAP).astype(F32)
    table_ref[...] = chosen.astype(BF16)


def slot_tables(expert_ids, gate_codes, lengths, experts):
    tok_count = expert_ids.shape[0]
    row_count = experts * 2 * SIDE * CAP
    return pl.pallas_call(
        table_kernel,
        in_specs=[SMEM, VMEM, VMEM],
        out_shape=[
            shape(row_count, 2 * SIDE * tok_count),
            shape(row_count, 128, dtype=F32),
            shape(experts * SIDE * CAP, tok_count),
        ],
        compiler_params=PARAMS,
        name="slot_tables",
    )(lengths, expert_ids.T, gate_codes.T)


def select_kernel(rows_ref, scale_ref, tokens_ref, grads_ref, out_ref):
    tok_count = tokens_ref.shape[0]
    part = out_ref.shape[1]
    total = None
    for q in range(SIDE):
        span = slice(q * part, (q + 1) * part)
        for array, ref in enumerate((tokens_ref, grads_ref)):
            p = 2 * q + array
            term = dot(
                rows_ref[:, p * tok_count : (p + 1) * tok_count], ref[:, span], NN
            )
            total = term if total is None else total + term
    out_ref[...] = (scale_ref[:, :1] * total).astype(BF16)


def select_rows(rows, scale, tokens, grad_out):
    return pl.pallas_call(
        select_kernel,
        in_specs=[VMEM] * 4,
        out_shape=shape(rows.shape[0], tokens.shape[1] // SIDE),
        compiler_params=PARAMS,
        name="select_rows",
    )(rows, scale, tokens, grad_out)


def exchange(x, experts):
    folded, width = x.shape
    blocks = x.reshape(experts, folded // experts, width)
    return lax.all_to_all(
        blocks, ("grp", "sp"), split_axis=0, concat_axis=0, tiled=True
    ).reshape(folded, width)


def unfold_kernel(a_ref, x_ref, *refs):
    out_refs = refs[-SIDE:]
    rows, folded = out_refs[0].shape[0], x_ref.shape[0]
    part = x_ref.shape[1]
    to = lax.broadcasted_iota(jnp.int32, (rows, folded), 0)
    src = lax.broadcasted_iota(jnp.int32, (rows, folded), 1)
    first = (to // CAP) * (2 * SIDE * CAP) + to % CAP
    for d, out_ref in enumerate(out_refs):
        quarter = (a_ref[0] + d) % SIDE
        for array in range(2):
            pick = (src == first + (quarter * 2 + array) * CAP).astype(BF16)
            out_ref[:, array * part : (array + 1) * part] = dot(
                pick, x_ref[...], NN
            ).astype(BF16)


def unfold(a, x, after):
    folded, part = x.shape
    rows = folded // (2 * SIDE)
    return pl.pallas_call(
        unfold_kernel,
        in_specs=[SMEM, VMEM] + [ANY] * len(after),
        out_shape=[shape(rows, 2 * part)] * SIDE,
        compiler_params=PARAMS,
        name="unfold",
    )(a, x, *after)


def line_kernel(a_ref, *refs):
    out_ref = refs[-1]
    for d, x_ref in enumerate(refs[:SIDE]):
        rows = x_ref.shape[0]
        at = ((a_ref[0] + SIDE - d) % SIDE) * rows
        out_ref[pl.ds(pl.multiple_of(at, 16), rows), :] = x_ref[...]


def line_up(a, blocks, after):
    rows, width = blocks[0].shape
    return pl.pallas_call(
        line_kernel,
        in_specs=[SMEM] + [VMEM] * SIDE + [ANY] * len(after),
        out_shape=shape(SIDE * rows, width),
        compiler_params=PARAMS,
        name="line_up",
    )(a, *blocks, *after)


def forward_kernel(count, *refs):
    pieces, weights, outs = refs[:count], refs[count : count + SIDE], refs[-SIDE:]
    part = weights[0].shape[0]
    units = weights[0].shape[1] // 3
    at = 0
    for piece in pieces:
        span = slice(at, at + piece.shape[0])
        at += piece.shape[0]
        for weight, out in zip(weights, outs):
            inner = dot(piece[:, :part], weight[:, : 2 * units], NN)
            out[span, : 2 * units] = inner.astype(out.dtype)
            outer = dot(piece[:, part:], weight[:, 2 * units :], NN)
            out[span, 2 * units :] = outer.astype(out.dtype)


def forward(pieces, weights, after):
    rows = sum(piece.shape[0] for piece in pieces)
    part, columns = weights[0].shape
    return pl.pallas_call(
        functools.partial(forward_kernel, len(pieces)),
        in_specs=[VMEM] * (len(pieces) + SIDE) + [ANY] * len(after),
        out_shape=[shape(rows, columns, dtype=F32)] + [shape(rows, columns)] * (SIDE - 1),
        compiler_params=PARAMS,
        cost_estimate=pl.CostEstimate(
            flops=2 * SIDE * rows * part * columns,
            bytes_accessed=4 * rows * part + 2 * SIDE * (part + rows) * columns,
            transcendentals=0,
        ),
        name="forward",
    )(*pieces, *weights, *after)


def activate_kernel(*refs):
    terms, out_ref = refs[:-1], refs[-1]
    total = terms[0][...]
    for term in terms[1:]:
        total = total + term[...].astype(F32)
    units = total.shape[1] // 3
    gate_pre, up_pre, hidden_grad = (
        total[:, :units], total[:, units : 2 * units], total[:, 2 * units :],
    )
    logistic = 1.0 / (1.0 + jnp.exp(-gate_pre))
    out_ref[:, :units] = (gate_pre * logistic * up_pre).astype(BF16)
    out_ref[:, units : 2 * units] = (
        hidden_grad * up_pre * logistic * (1.0 + gate_pre * (1.0 - logistic))
    ).astype(BF16)
    out_ref[:, 2 * units :] = (hidden_grad * gate_pre * logistic).astype(BF16)


def activate(terms):
    return pl.pallas_call(
        activate_kernel,
        in_specs=[VMEM] * SIDE,
        out_shape=shape(*terms[0].shape),
        compiler_params=PARAMS,
        name="activate",
    )(*terms)


def backward_kernel(count, *refs):
    hidden, weights, outs = refs[:SIDE], refs[SIDE : 2 * SIDE], refs[-count:]
    rows = outs[0].shape[0]
    units = hidden[0].shape[1] // 3
    for i, out in enumerate(outs):
        span = slice(i * rows, (i + 1) * rows)
        total = None
        for h, weight in zip(hidden, weights):
            term = dot(h[span, units:], weight[:, : 2 * units], NT)
            total = term if total is None else total + term
        out[...] = total.astype(out.dtype)


def backward(hidden, weights, dtypes, after):
    rows = hidden[0].shape[0] // len(dtypes)
    part, columns = weights[0].shape
    return pl.pallas_call(
        functools.partial(backward_kernel, len(dtypes)),
        in_specs=[VMEM] * (2 * SIDE) + [ANY] * len(after),
        out_shape=[shape(rows, part, dtype=dtype) for dtype in dtypes],
        compiler_params=PARAMS,
        cost_estimate=pl.CostEstimate(
            flops=2 * SIDE * rows * len(dtypes) * part * columns * 2 // 3,
            bytes_accessed=2 * SIDE * (part + rows * len(dtypes)) * columns,
            transcendentals=0,
        ),
        name="backward",
    )(*hidden, *weights, *after)


def weight_kernel(layout, *refs):
    count = sum(layout)
    pieces, hidden, out_ref = refs[:count], refs[count : count + len(layout)], refs[-1]
    part = out_ref.shape[0]
    units = out_ref.shape[1] // 3
    inner, outer, i = None, None, 0
    for h, members in zip(hidden, layout):
        at = 0
        for piece in pieces[i : i + members]:
            span = slice(at, at + piece.shape[0])
            at += piece.shape[0]
            term = dot(piece[:, :part], h[span, units:], TN)
            inner = term if inner is None else inner + term
            term = dot(piece[:, part:], h[span, :units], TN)
            outer = term if outer is None else outer + term
        i += members
    out_ref[:, : 2 * units] = inner.astype(BF16)
    out_ref[:, 2 * units :] = outer.astype(BF16)


def weight_grads(chunks, hidden, after):
    pieces = [piece for chunk in chunks for piece in chunk]
    part = pieces[0].shape[1] // 2
    columns = hidden[0].shape[1]
    rows = sum(piece.shape[0] for piece in pieces)
    return pl.pallas_call(
        functools.partial(weight_kernel, tuple(len(chunk) for chunk in chunks)),
        in_specs=[VMEM] * (len(pieces) + len(hidden)) + [ANY] * len(after),
        out_shape=shape(part, columns),
        compiler_params=PARAMS,
        cost_estimate=pl.CostEstimate(
            flops=2 * rows * part * columns,
            bytes_accessed=4 * rows * part + 2 * (part + rows) * columns,
            transcendentals=0,
        ),
        name="weight_grads",
    )(*pieces, *hidden, *after)


def unpack_kernel(quarter_ref, x_ref, *refs):
    gate_ref, up_ref, down_ref, mark_ref = refs[-4:]
    units = gate_ref.shape[1]
    mark_ref[...] = jnp.zeros_like(mark_ref)
    gate_ref[...] = x_ref[:, :units]
    up_ref[...] = x_ref[:, units : 2 * units]
    down_ref[...] = x_ref[:, 2 * units :].T


def unpack(quarter, x, into):
    part, columns = x.shape
    units, width = columns // 3, part * SIDE
    tile = part // 2
    earlier = [] if into is None else list(into)
    return pl.pallas_call(
        unpack_kernel,
        grid_spec=pltpu.PrefetchScalarGridSpec(
            num_scalar_prefetch=1,
            grid=(2,),
            in_specs=[pl.BlockSpec((tile, columns), lambda j, q: (j, 0))]
            + [pl.BlockSpec(memory_space=pl.ANY)] * len(earlier),
            out_specs=[
                pl.BlockSpec((tile, units), lambda j, q: (q[0] * 2 + j, 0)),
                pl.BlockSpec((tile, units), lambda j, q: (q[0] * 2 + j, 0)),
                pl.BlockSpec((units, tile), lambda j, q: (0, q[0] * 2 + j)),
                pl.BlockSpec((8, 128), lambda j, q: (0, 0)),
            ],
        ),
        out_shape=[
            shape(width, units),
            shape(width, units),
            shape(units, width),
            shape(8, 128, dtype=F32),
        ],
        input_output_aliases={2 + i: i for i in range(len(earlier))},
        compiler_params=PARAMS,
        name="unpack",
    )(quarter, x, *earlier)


def sum_kernel(a_ref, *refs):
    terms, outs = refs[:SIDE], refs[-SIDE:]
    rows = outs[0].shape[0]
    for d, out in enumerate(outs):
        at = pl.multiple_of(((a_ref[0] + d) % SIDE) * rows, 16)
        total = None
        for term in terms:
            x = term[pl.ds(at, rows), :].astype(F32)
            total = x if total is None else total + x
        out[...] = total.astype(BF16)


def sum_rows(a, terms, after):
    rows, part = terms[0].shape
    return pl.pallas_call(
        sum_kernel,
        in_specs=[SMEM] + [VMEM] * SIDE + [ANY] * len(after),
        out_shape=[shape(rows // SIDE, part)] * SIDE,
        compiler_params=PARAMS,
        name="sum_rows",
    )(a, *terms, *after)


def halve_kernel(first_ref, second_ref, *refs):
    head_ref, tail_ref = refs[-2:]
    half = head_ref.shape[0]
    head_ref[...] = first_ref[:half, :]
    tail_ref[...] = second_ref[half:, :]


def halve(first, second, after):
    rows, width = first.shape
    return pl.pallas_call(
        halve_kernel,
        in_specs=[VMEM, VMEM] + [ANY] * len(after),
        out_shape=[shape(rows // 2, width)] * 2,
        compiler_params=PARAMS,
        name="halve",
    )(first, second, *after)


def fold_kernel(a_ref, *refs):
    blocks, out_ref = refs[:SIDE], refs[len(refs) - (len(refs) - SIDE + 1) // 2]
    folded, rows = out_ref.shape[0], blocks[0].shape[0]
    to = lax.broadcasted_iota(jnp.int32, (folded, rows), 0)
    src = lax.broadcasted_iota(jnp.int32, (folded, rows), 1)
    first = (src // CAP) * (SIDE * CAP) + src % CAP
    total = None
    for d, x_ref in enumerate(blocks):
        quarter = (a_ref[0] + SIDE - d) % SIDE
        term = dot((to == first + quarter * CAP).astype(BF16), x_ref[...], NN)
        total = term if total is None else total + term
    out_ref[...] = total.astype(BF16)


def fold(a, blocks, held):
    rows, part = blocks[0].shape
    return pl.pallas_call(
        fold_kernel,
        in_specs=[SMEM] + [VMEM] * SIDE + [ANY] * len(held),
        out_specs=[VMEM] + [ANY] * len(held),
        out_shape=[shape(rows * SIDE, part)] + [shape(*x.shape) for x in held],
        input_output_aliases={1 + SIDE + i: 1 + i for i in range(len(held))},
        compiler_params=PARAMS,
        name="fold",
    )(a, *blocks, *held)


def combine_kernel(table_ref, x_ref, out_ref):
    table = table_ref[...]
    row = lax.broadcasted_iota(jnp.int32, table.shape, 0)
    quarter = pl.program_id(0)
    mine = jnp.where((row // CAP) % SIDE == quarter, table, jnp.zeros_like(table))
    out_ref[...] = dot(mine, x_ref[...], TN).astype(BF16)


def combine(table, x):
    folded, part = x.shape
    tok_count = table.shape[1]
    return pl.pallas_call(
        combine_kernel,
        grid=(SIDE,),
        in_specs=[
            pl.BlockSpec(table.shape, lambda q: (0, 0)),
            pl.BlockSpec((folded, part), lambda q: (0, 0)),
        ],
        out_specs=pl.BlockSpec((tok_count, part), lambda q: (0, q)),
        out_shape=shape(tok_count, part * SIDE),
        compiler_params=PARAMS,
        name="combine",
    )(table, x)


def body(tokens, grad_out, expert_ids, gate_codes, lengths, w_gate, w_up, w_down):
    experts = lax.axis_size("grp") * lax.axis_size("sp")
    dp = lax.axis_index("dp")
    a = jnp.where(lax.axis_index("grp") == 0, dp % SIDE, dp // SIDE).astype(jnp.int32)[None]
    quarters = [(a + d) % SIDE for d in range(SIDE)]
    gate_w, up_w, down_w = w_gate[0], w_up[0], w_down[0]

    rows, scale, table = slot_tables(expert_ids, gate_codes, lengths, experts)
    sent = select_rows(rows, scale, tokens, grad_out)
    packed = pack_weights(a, gate_w, up_w, down_w)
    weights = [packed[0]] + [shift(packed[d], True, d) for d in range(1, SIDE)]

    blocks = unfold(a, exchange(sent, experts), weights[1:])
    blocks = [blocks[0]] + [shift(blocks[d], True, d) for d in range(1, SIDE)]
    line = line_up(a, blocks, [])
    after, before = shift(line, False, 1), shift(line, False, -1)

    def presums(pieces, after):
        terms = forward(pieces, weights, after)
        return [terms[0]] + [shift(terms[d], True, -d) for d in range(1, SIDE)]

    def spread(acts):
        return [acts] + [shift(acts, True, d) for d in range(1, SIDE)]

    head, tail = halve(after, before, [])
    far = [shift(head, False, 1), shift(tail, False, -1)]
    terms = presums([line, after, before], [])
    first = terms[0]
    most = spread(activate(terms))
    last = spread(activate(presums(far, [most[0]])))
    hidden = [most, last]
    chunks = [[line, after, before], far]

    across = weight_grads(
        chunks, [most[2], last[2]], [most[1], most[3], last[1], last[3]]
    )
    own, to_before, to_after = backward(most, weights, [F32, BF16, BF16], [last[1], across])
    (to_far,) = backward(last, weights, [BF16], [to_before])
    row_terms = [
        own,
        shift(to_before, False, -1),
        shift(to_after, False, 1),
        shift(to_far, False, 2),
    ]

    def grads_of(d, after):
        return weight_grads(chunks, [chunk[d] for chunk in hidden], after)

    *into, mark = unpack(quarters[0], grads_of(0, [to_far]), None)
    *into, mark = unpack(quarters[2], shift(across, True, -2), into)
    grads = [grads_of(d, [to_far]) for d in (1, 3)]
    parts = sum_rows(a, row_terms, [mark] + grads)
    returned = [parts[0]] + [shift(parts[d], True, d) for d in range(1, SIDE)]
    folded, *grads = fold(a, returned, grads)
    grad_tokens = combine(table, exchange(folded, experts))
    for d, x in zip((1, 3), grads):
        *into, _ = unpack(quarters[d], shift(x, True, -d), into)
    gate_w_grad, up_w_grad, down_w_grad = into
    return (grad_tokens, gate_w_grad[None], up_w_grad[None], down_w_grad[None])


def solution(mesh):
    return jax.shard_map(
        body,
        mesh=mesh,
        in_specs=(
            P(("grp", "dp", "sp"), None),
            P(("grp", "dp", "sp"), None),
            P(("grp", "dp", "sp"), None),
            P(("grp", "dp", "sp"), None),
            P(("grp", "dp", "sp"), None),
            P(("grp", "sp"), None, "dp"),
            P(("grp", "sp"), None, "dp"),
            P(("grp", "sp"), "dp", None),
        ),
        out_specs=(
            P(("grp", "dp", "sp"), None),
            P(("grp", "sp"), None, "dp"),
            P(("grp", "sp"), None, "dp"),
            P(("grp", "sp"), "dp", None),
        ),
        check_vma=False,
    )
```

```python
import functools

import jax
import jax.numpy as jnp
from jax import lax
from jax.experimental import pallas as pl
from jax.experimental.pallas import tpu as pltpu
from jax.sharding import PartitionSpec as P

CAP = 6
SIDE = 4
GRID_SCALE = 2048.0
BF16 = jnp.bfloat16
F32 = jnp.float32
MIB = 1024 * 1024
PARAMS = pltpu.CompilerParams(vmem_limit_bytes=24 * MIB)
SMEM = pl.BlockSpec(memory_space=pltpu.SMEM)
VMEM = pl.BlockSpec(memory_space=pltpu.VMEM)
ANY = pl.BlockSpec(memory_space=pl.ANY)


def dot(a, b, contract):
    return lax.dot_general(a, b, (contract, ((), ())), preferred_element_type=F32)


NN = ((1,), (0,))
NT = ((1,), (1,))
TN = ((0,), (0,))


def shape(*dims, dtype=BF16):
    return jax.ShapeDtypeStruct(dims, dtype)


def shift(x, along_a, step):
    pairs = []
    for grp in range(2):
        for y in range(SIDE):
            for z in range(SIDE):
                if (grp == 0) == along_a:
                    to = (y, (z + step) % SIDE)
                else:
                    to = ((y + step) % SIDE, z)
                pairs.append(
                    (grp * SIDE * SIDE + y * SIDE + z, grp * SIDE * SIDE + to[0] * SIDE + to[1])
                )
    return lax.ppermute(x, ("grp", "dp"), pairs)


def pack_kernel(a_ref, gate_ref, up_ref, down_ref, *refs):
    outs, down, sems = refs[:SIDE], refs[SIDE], refs[SIDE + 1]
    part, units = outs[0].shape[0], down.shape[0]
    starts = [
        pl.multiple_of(((a_ref[0] + d) % SIDE) * part, 128) for d in range(SIDE)
    ]
    load = pltpu.make_async_copy(down_ref, down, sems.at[2 * SIDE])
    load.start()
    copies = []
    for d in (1, 3, 2, 0):
        for k, ref in enumerate((gate_ref, up_ref)):
            copy = pltpu.make_async_copy(
                ref.at[pl.ds(starts[d], part), :],
                outs[d].at[:, pl.ds(k * units, units)],
                sems.at[2 * d + k],
            )
            copy.start()
            copies.append(copy)
    load.wait()
    for d, out_ref in enumerate(outs):
        out_ref[:, 2 * units :] = down[:, pl.ds(starts[d], part)].T
    for copy in copies:
        copy.wait()


def pack_weights(a, gate_w, up_w, down_w):
    width, units = gate_w.shape
    return pl.pallas_call(
        pack_kernel,
        in_specs=[SMEM, ANY, ANY, ANY],
        out_shape=[shape(width // SIDE, 3 * units)] * SIDE,
        scratch_shapes=[
            pltpu.VMEM((units, width), BF16),
            pltpu.SemaphoreType.DMA((2 * SIDE + 1,)),
        ],
        compiler_params=PARAMS,
        name="pack_weights",
    )(a, gate_w, up_w, down_w)


def table_kernel(lengths_ref, ids_ref, codes_ref, rows_ref, scale_ref, table_ref):
    experts, tok_count = ids_ref.shape
    folded = 2 * SIDE * CAP
    row_count = experts * folded
    ids = ids_ref[...]
    codes = codes_ref[...]
    slot_len = tok_count // 2
    position = lax.broadcasted_iota(jnp.int32, (1, tok_count), 1)
    bound = jnp.where(position < slot_len, lengths_ref[0, 0], lengths_ref[0, 1] + slot_len)
    live = position < bound
    expert = lax.broadcasted_iota(jnp.int32, (experts, tok_count), 0)
    member = jnp.zeros((experts, tok_count), F32)
    gate = jnp.zeros((experts, tok_count), F32)
    for e in range(experts):
        hit = ids == e
        found = jnp.sum(hit.astype(F32), axis=0, keepdims=True)
        code = jnp.sum(jnp.where(hit, codes, 0).astype(F32), axis=0, keepdims=True)
        here = jnp.logical_and(live, found > 0.0)
        member = jnp.where(jnp.logical_and(expert == e, here), 1.0, member)
        gate = jnp.where(expert == e, code / GRID_SCALE, gate)
    earlier = lax.broadcasted_iota(jnp.int32, (tok_count, tok_count), 0)
    later = lax.broadcasted_iota(jnp.int32, (tok_count, tok_count), 1)
    rank = dot(member.astype(BF16), (earlier < later).astype(BF16), NN)
    slot_of = jnp.where(member > 0.0, rank, -1.0)

    def spread(x, times):
        return jnp.broadcast_to(x[:, None, :], (experts, times, tok_count)).reshape(
            experts * times, tok_count
        )

    row = lax.broadcasted_iota(jnp.int32, (row_count, tok_count), 0)
    chosen = spread(slot_of, folded) == (row % CAP).astype(F32)
    part = (row // CAP) % (2 * SIDE)
    for p in range(2 * SIDE):
        mine = jnp.logical_and(chosen, part == p)
        rows_ref[:, p * tok_count : (p + 1) * tok_count] = mine.astype(BF16)
    weight = jnp.sum(jnp.where(chosen, spread(gate, folded), 0.0), axis=1, keepdims=True)
    is_grad = (part % 2)[:, :1] == 1
    scale_ref[...] = jnp.broadcast_to(jnp.where(is_grad, weight, 1.0), scale_ref.shape)
    row = lax.broadcasted_iota(jnp.int32, table_ref.shape, 0)
    chosen = spread(slot_of, SIDE * CAP) == (row % CAP).astype(F32)
    table_ref[...] = chosen.astype(BF16)


def slot_tables(expert_ids, gate_codes, lengths, experts):
    tok_count = expert_ids.shape[0]
    row_count = experts * 2 * SIDE * CAP
    return pl.pallas_call(
        table_kernel,
        in_specs=[SMEM, VMEM, VMEM],
        out_shape=[
            shape(row_count, 2 * SIDE * tok_count),
            shape(row_count, 128, dtype=F32),
            shape(experts * SIDE * CAP, tok_count),
        ],
        compiler_params=PARAMS,
        name="slot_tables",
    )(lengths, expert_ids.T, gate_codes.T)


def select_kernel(rows_ref, scale_ref, tokens_ref, grads_ref, out_ref):
    tok_count = tokens_ref.shape[0]
    part = out_ref.shape[1]
    total = None
    for q in range(SIDE):
        span = slice(q * part, (q + 1) * part)
        for array, ref in enumerate((tokens_ref, grads_ref)):
            p = 2 * q + array
            term = dot(
                rows_ref[:, p * tok_count : (p + 1) * tok_count], ref[:, span], NN
            )
            total = term if total is None else total + term
    out_ref[...] = (scale_ref[:, :1] * total).astype(BF16)


def select_rows(rows, scale, tokens, grad_out):
    return pl.pallas_call(
        select_kernel,
        in_specs=[VMEM] * 4,
        out_shape=shape(rows.shape[0], tokens.shape[1] // SIDE),
        compiler_params=PARAMS,
        name="select_rows",
    )(rows, scale, tokens, grad_out)


def exchange(x, experts):
    folded, width = x.shape
    blocks = x.reshape(experts, folded // experts, width)
    return lax.all_to_all(
        blocks, ("grp", "sp"), split_axis=0, concat_axis=0, tiled=True
    ).reshape(folded, width)


def unfold_kernel(a_ref, x_ref, *refs):
    out_refs = refs[-SIDE:]
    rows, folded = out_refs[0].shape[0], x_ref.shape[0]
    part = x_ref.shape[1]
    to = lax.broadcasted_iota(jnp.int32, (rows, folded), 0)
    src = lax.broadcasted_iota(jnp.int32, (rows, folded), 1)
    first = (to // CAP) * (2 * SIDE * CAP) + to % CAP
    for d, out_ref in enumerate(out_refs):
        quarter = (a_ref[0] + d) % SIDE
        for array in range(2):
            pick = (src == first + (quarter * 2 + array) * CAP).astype(BF16)
            out_ref[:, array * part : (array + 1) * part] = dot(
                pick, x_ref[...], NN
            ).astype(BF16)


def unfold(a, x, after):
    folded, part = x.shape
    rows = folded // (2 * SIDE)
    return pl.pallas_call(
        unfold_kernel,
        in_specs=[SMEM, VMEM] + [ANY] * len(after),
        out_shape=[shape(rows, 2 * part)] * SIDE,
        compiler_params=PARAMS,
        name="unfold",
    )(a, x, *after)


def line_kernel(a_ref, *refs):
    halves = refs[-2:]
    for d, x_ref in enumerate(refs[:SIDE]):
        rows = x_ref.shape[0]
        place = (a_ref[0] + SIDE - d) % SIDE
        at = pl.multiple_of((place % 2) * rows, 16)
        for h, out_ref in enumerate(halves):

            @pl.when(place // 2 == h)
            def _(x_ref=x_ref, out_ref=out_ref, at=at, rows=rows):
                out_ref[pl.ds(at, rows), :] = x_ref[...]


def line_up(a, blocks):
    rows, width = blocks[0].shape
    return pl.pallas_call(
        line_kernel,
        in_specs=[SMEM] + [VMEM] * SIDE,
        out_shape=[shape(SIDE // 2 * rows, width)] * 2,
        compiler_params=PARAMS,
        name="line_up",
    )(a, *blocks)


def join_kernel(first_ref, second_ref, third_ref, fourth_ref, up_ref, down_ref):
    half = first_ref.shape[0]
    up_ref[:half, :] = first_ref[...]
    up_ref[half:, :] = second_ref[...]
    down_ref[:half, :] = third_ref[...]
    down_ref[half:, :] = fourth_ref[...]


def join(*halves):
    rows, width = halves[0].shape
    return pl.pallas_call(
        join_kernel,
        in_specs=[VMEM] * 4,
        out_shape=[shape(2 * rows, width)] * 2,
        compiler_params=PARAMS,
        name="join",
    )(*halves)


def forward_kernel(count, *refs):
    pieces, weights, outs = refs[:count], refs[count : count + SIDE], refs[-SIDE:]
    part = weights[0].shape[0]
    units = weights[0].shape[1] // 3
    at = 0
    for piece in pieces:
        span = slice(at, at + piece.shape[0])
        at += piece.shape[0]
        for weight, out in zip(weights, outs):
            inner = dot(piece[:, :part], weight[:, : 2 * units], NN)
            out[span, : 2 * units] = inner.astype(out.dtype)
            outer = dot(piece[:, part:], weight[:, 2 * units :], NN)
            out[span, 2 * units :] = outer.astype(out.dtype)


def forward(pieces, weights, after):
    rows = sum(piece.shape[0] for piece in pieces)
    part, columns = weights[0].shape
    return pl.pallas_call(
        functools.partial(forward_kernel, len(pieces)),
        in_specs=[VMEM] * (len(pieces) + SIDE) + [ANY] * len(after),
        out_shape=[shape(rows, columns, dtype=F32)] + [shape(rows, columns)] * (SIDE - 1),
        compiler_params=PARAMS,
        cost_estimate=pl.CostEstimate(
            flops=2 * SIDE * rows * part * columns,
            bytes_accessed=4 * rows * part + 2 * SIDE * (part + rows) * columns,
            transcendentals=0,
        ),
        name="forward",
    )(*pieces, *weights, *after)


def activate_kernel(*refs):
    out_ref = refs[-1]
    units = out_ref.shape[1] // 3
    at = 0
    for g in range(0, len(refs) - 1, SIDE):
        total = refs[g][...]
        for term in refs[g + 1 : g + SIDE]:
            total = total + term[...].astype(F32)
        span = slice(at, at + total.shape[0])
        at += total.shape[0]
        gate_pre, up_pre, hidden_grad = (
            total[:, :units], total[:, units : 2 * units], total[:, 2 * units :],
        )
        logistic = 1.0 / (1.0 + jnp.exp(-gate_pre))
        out_ref[span, :units] = (gate_pre * logistic * up_pre).astype(BF16)
        out_ref[span, units : 2 * units] = (
            hidden_grad * up_pre * logistic * (1.0 + gate_pre * (1.0 - logistic))
        ).astype(BF16)
        out_ref[span, 2 * units :] = (hidden_grad * gate_pre * logistic).astype(BF16)


def activate(groups):
    rows = sum(terms[0].shape[0] for terms in groups)
    return pl.pallas_call(
        activate_kernel,
        in_specs=[VMEM] * (SIDE * len(groups)),
        out_shape=shape(rows, groups[0][0].shape[1]),
        compiler_params=PARAMS,
        name="activate",
    )(*[term for terms in groups for term in terms])


def backward_kernel(blocks, *refs):
    chunks = (refs[:SIDE], refs[SIDE : 2 * SIDE])
    weights, outs = refs[2 * SIDE : 3 * SIDE], refs[-len(blocks) :]
    units = weights[0].shape[1] // 3
    for block, out in zip(blocks, outs):
        rows = out.shape[0] // 2
        for k, half in enumerate(block):
            at = half % SIDE * rows
            total = None
            for h, weight in zip(chunks[half // SIDE], weights):
                term = dot(h[at : at + rows, units:], weight[:, : 2 * units], NT)
                total = term if total is None else total + term
            out[k * rows : (k + 1) * rows, :] = total.astype(out.dtype)


def backward(hidden, weights, blocks, dtype, after):
    rows = hidden[0][0].shape[0] // 2
    part, columns = weights[0].shape
    return pl.pallas_call(
        functools.partial(backward_kernel, blocks),
        in_specs=[VMEM] * (3 * SIDE) + [ANY] * len(after),
        out_shape=[shape(rows, part, dtype=dtype) for _ in blocks],
        compiler_params=PARAMS,
        cost_estimate=pl.CostEstimate(
            flops=2 * SIDE * rows * len(blocks) * part * columns * 2 // 3,
            bytes_accessed=2 * SIDE * (part + rows * len(blocks)) * columns,
            transcendentals=0,
        ),
        name="backward",
    )(*hidden[0], *hidden[1], *weights, *after)


def weight_kernel(layout, *refs):
    count = sum(layout)
    pieces, chunks, out_ref = refs[:count], refs[count : count + len(layout)], refs[-1]
    units = out_ref.shape[1]
    part = out_ref.shape[0] // 3
    inner, outer, i = None, None, 0
    for hidden, members in zip(chunks, layout):
        at = 0
        for piece in pieces[i : i + members]:
            span = slice(at, at + piece.shape[0])
            at += piece.shape[0]
            term = dot(piece[:, :part], hidden[span, units:], TN)
            inner = term if inner is None else inner + term
            term = dot(hidden[span, :units], piece[:, part:], TN)
            outer = term if outer is None else outer + term
        i += members
    out_ref[:part, :] = inner[:, :units].astype(BF16)
    out_ref[part : 2 * part, :] = inner[:, units:].astype(BF16)
    for k in range(part // units):
        out_ref[2 * part + k * units : 2 * part + (k + 1) * units, :] = outer[
            :, k * units : (k + 1) * units
        ].astype(BF16)


def weight_grads(groups, hidden, after):
    pieces = [piece for group in groups for piece in group]
    part = pieces[0].shape[1] // 2
    columns = hidden[0].shape[1]
    rows = sum(h.shape[0] for h in hidden)
    return pl.pallas_call(
        functools.partial(weight_kernel, tuple(len(group) for group in groups)),
        in_specs=[VMEM] * (len(pieces) + len(hidden)) + [ANY] * len(after),
        out_shape=shape(3 * part, columns // 3),
        compiler_params=PARAMS,
        cost_estimate=pl.CostEstimate(
            flops=2 * rows * part * columns,
            bytes_accessed=4 * rows * part + 2 * (part + rows) * columns,
            transcendentals=0,
        ),
        name="weight_grads",
    )(*pieces, *hidden, *after)


def unpack_kernel(steps, a_ref, *refs):
    count = len(steps)
    gate_ref, up_ref, down_ref, mark_ref, sems = refs[-5:]
    units = gate_ref.shape[1]
    part = gate_ref.shape[0] // SIDE
    copies = []
    for i, (step, x_ref) in enumerate(zip(steps, refs[:count])):
        quarter = (a_ref[0] + step) % SIDE
        at = pl.multiple_of(quarter * part, 128)
        pairs = [
            (x_ref.at[pl.ds(0, part), :], gate_ref.at[pl.ds(at, part), :]),
            (x_ref.at[pl.ds(part, part), :], up_ref.at[pl.ds(at, part), :]),
        ]
        for k in range(part // units):
            pairs.append(
                (
                    x_ref.at[pl.ds(2 * part + k * units, units), :],
                    down_ref.at[:, pl.ds(pl.multiple_of(at + k * units, 128), units)],
                )
            )
        for k, (source, target) in enumerate(pairs):
            copy = pltpu.make_async_copy(source, target, sems.at[i, k])
            copy.start()
            copies.append(copy)
    mark_ref[...] = jnp.zeros_like(mark_ref)
    for copy in copies:
        copy.wait()


def unpack(a, steps, arrays, into):
    rows, units = arrays[0].shape
    part = rows // 3
    width = part * SIDE
    earlier = [] if into is None else list(into)
    return pl.pallas_call(
        functools.partial(unpack_kernel, steps),
        in_specs=[SMEM] + [ANY] * (len(arrays) + len(earlier)),
        out_specs=[ANY, ANY, ANY, VMEM],
        out_shape=[
            shape(width, units),
            shape(width, units),
            shape(units, width),
            shape(8, 128, dtype=F32),
        ],
        scratch_shapes=[pltpu.SemaphoreType.DMA((len(arrays), 2 + part // units))],
        input_output_aliases={1 + len(arrays) + i: i for i in range(len(earlier))},
        compiler_params=PARAMS,
        name="unpack",
    )(a, *arrays, *earlier)


def sum_kernel(a_ref, *refs):
    terms, outs = refs[:SIDE], refs[-SIDE:]
    rows = outs[0].shape[0]
    for d, out in enumerate(outs):
        at = pl.multiple_of(((a_ref[0] + d) % SIDE) * rows, 16)
        total = None
        for term in terms:
            x = term[pl.ds(at, rows), :].astype(F32)
            total = x if total is None else total + x
        out[...] = total.astype(BF16)


def sum_rows(a, terms, after):
    rows, part = terms[0].shape
    return pl.pallas_call(
        sum_kernel,
        in_specs=[SMEM] + [VMEM] * SIDE + [ANY] * len(after),
        out_shape=[shape(rows // SIDE, part)] * SIDE,
        compiler_params=PARAMS,
        name="sum_rows",
    )(a, *terms, *after)


def fold_kernel(a_ref, *refs):
    blocks, out_ref = refs[:SIDE], refs[len(refs) - (len(refs) - SIDE + 1) // 2]
    folded, rows = out_ref.shape[0], blocks[0].shape[0]
    to = lax.broadcasted_iota(jnp.int32, (folded, rows), 0)
    src = lax.broadcasted_iota(jnp.int32, (folded, rows), 1)
    first = (src // CAP) * (SIDE * CAP) + src % CAP
    total = None
    for d, x_ref in enumerate(blocks):
        quarter = (a_ref[0] + SIDE - d) % SIDE
        term = dot((to == first + quarter * CAP).astype(BF16), x_ref[...], NN)
        total = term if total is None else total + term
    out_ref[...] = total.astype(BF16)


def fold(a, blocks, held):
    rows, part = blocks[0].shape
    return pl.pallas_call(
        fold_kernel,
        in_specs=[SMEM] + [VMEM] * SIDE + [ANY] * len(held),
        out_specs=[VMEM] + [ANY] * len(held),
        out_shape=[shape(rows * SIDE, part)] + [shape(*x.shape) for x in held],
        input_output_aliases={1 + SIDE + i: 1 + i for i in range(len(held))},
        compiler_params=PARAMS,
        name="fold",
    )(a, *blocks, *held)


def combine_kernel(table_ref, x_ref, out_ref):
    table = table_ref[...]
    row = lax.broadcasted_iota(jnp.int32, table.shape, 0)
    quarter = pl.program_id(0)
    mine = jnp.where((row // CAP) % SIDE == quarter, table, jnp.zeros_like(table))
    out_ref[...] = dot(mine, x_ref[...], TN).astype(BF16)


def combine(table, x):
    folded, part = x.shape
    tok_count = table.shape[1]
    return pl.pallas_call(
        combine_kernel,
        grid=(SIDE,),
        in_specs=[
            pl.BlockSpec(table.shape, lambda q: (0, 0)),
            pl.BlockSpec((folded, part), lambda q: (0, 0)),
        ],
        out_specs=pl.BlockSpec((tok_count, part), lambda q: (0, q)),
        out_shape=shape(tok_count, part * SIDE),
        compiler_params=PARAMS,
        name="combine",
    )(table, x)


def body(tokens, grad_out, expert_ids, gate_codes, lengths, w_gate, w_up, w_down):
    experts = lax.axis_size("grp") * lax.axis_size("sp")
    dp = lax.axis_index("dp")
    a = jnp.where(lax.axis_index("grp") == 0, dp % SIDE, dp // SIDE).astype(jnp.int32)[None]
    gate_w, up_w, down_w = w_gate[0], w_up[0], w_down[0]

    rows, scale, table = slot_tables(expert_ids, gate_codes, lengths, experts)
    sent = select_rows(rows, scale, tokens, grad_out)
    packed = pack_weights(a, gate_w, up_w, down_w)
    weights = [packed[0]] + [shift(packed[d], True, d) for d in range(1, SIDE)]

    blocks = unfold(a, exchange(sent, experts), weights[1:])
    blocks = [blocks[0]] + [shift(blocks[d], True, d) for d in range(1, SIDE)]
    head, tail = line_up(a, blocks)
    after_head, before_tail = shift(head, False, 1), shift(tail, False, -1)
    up, down = join(after_head, tail, before_tail, head)
    early = [head, tail, after_head, before_tail]
    late = [shift(up, False, 1), shift(down, False, -1)]

    def presums(pieces, after):
        terms = forward(pieces, weights, after)
        return [terms[0]] + [shift(terms[d], True, -d) for d in range(1, SIDE)]

    def spread(acts):
        return [acts] + [shift(acts, True, d) for d in range(1, SIDE)]

    most = presums(early, [])
    rest = presums(late, [most[0]])
    hidden = [spread(activate([most])), spread(activate([rest]))]
    groups = [early, late]

    own_rows, before_rows, after_rows, far_rows = (0, 1), (2, 5), (7, 3), (4, 6)

    def grads_of(d, after):
        return weight_grads(groups, [chunk[d] for chunk in hidden], after)

    across = grads_of(2, [chunk[d] for chunk in hidden for d in (1, 3)])
    (to_far,) = backward(hidden, weights, (far_rows,), BF16, [across])
    to_before, to_after = backward(
        hidden, weights, (before_rows, after_rows), BF16, [to_far]
    )
    (own,) = backward(hidden, weights, (own_rows,), F32, [to_after])
    row_terms = [
        own,
        shift(to_before, False, -1),
        shift(to_after, False, 1),
        shift(to_far, False, 2),
    ]
    *into, mark = unpack(a, (0,), [grads_of(0, [own])], None)
    grads = [grads_of(d, [own]) for d in (1, 3)]
    *into, mark = unpack(a, (2,), [shift(across, True, -2)], into)
    parts = sum_rows(a, row_terms, [mark] + grads)
    returned = [parts[0]] + [shift(parts[d], True, d) for d in range(1, SIDE)]
    folded, *grads = fold(a, returned, grads)
    grads = [shift(x, True, -d) for d, x in zip((1, 3), grads)]
    grad_tokens = combine(table, exchange(folded, experts))
    *into, _ = unpack(a, (1, 3), grads, into)
    gate_w_grad, up_w_grad, down_w_grad = into
    return (grad_tokens, gate_w_grad[None], up_w_grad[None], down_w_grad[None])


def solution(mesh):
    return jax.shard_map(
        body,
        mesh=mesh,
        in_specs=(
            P(("grp", "dp", "sp"), None),
            P(("grp", "dp", "sp"), None),
            P(("grp", "dp", "sp"), None),
            P(("grp", "dp", "sp"), None),
            P(("grp", "dp", "sp"), None),
            P(("grp", "sp"), None, "dp"),
            P(("grp", "sp"), None, "dp"),
            P(("grp", "sp"), "dp", None),
        ),
        out_specs=(
            P(("grp", "dp", "sp"), None),
            P(("grp", "sp"), None, "dp"),
            P(("grp", "sp"), None, "dp"),
            P(("grp", "sp"), "dp", None),
        ),
        check_vma=False,
    )
```

```python
import functools

import jax
import jax.numpy as jnp
from jax import lax
from jax.experimental import pallas as pl
from jax.experimental.pallas import tpu as pltpu
from jax.sharding import PartitionSpec as P

CAP = 6
SIDE = 4
GRID_SCALE = 2048.0
BF16 = jnp.bfloat16
F32 = jnp.float32
MIB = 1024 * 1024
PARAMS = pltpu.CompilerParams(vmem_limit_bytes=24 * MIB)
SMEM = pl.BlockSpec(memory_space=pltpu.SMEM)
VMEM = pl.BlockSpec(memory_space=pltpu.VMEM)
ANY = pl.BlockSpec(memory_space=pl.ANY)


def dot(a, b, contract):
    return lax.dot_general(a, b, (contract, ((), ())), preferred_element_type=F32)


NN = ((1,), (0,))
NT = ((1,), (1,))
TN = ((0,), (0,))


def shape(*dims, dtype=BF16):
    return jax.ShapeDtypeStruct(dims, dtype)


def shift(x, along_a, step):
    pairs = []
    for grp in range(2):
        for y in range(SIDE):
            for z in range(SIDE):
                if (grp == 0) == along_a:
                    to = (y, (z + step) % SIDE)
                else:
                    to = ((y + step) % SIDE, z)
                pairs.append(
                    (grp * SIDE * SIDE + y * SIDE + z, grp * SIDE * SIDE + to[0] * SIDE + to[1])
                )
    return lax.ppermute(x, ("grp", "dp"), pairs)


def pack_kernel(a_ref, gate_ref, up_ref, down_ref, *refs):
    outs, down, sems = refs[:SIDE], refs[SIDE], refs[SIDE + 1]
    part, units = outs[0].shape[0], down.shape[0]
    starts = [
        pl.multiple_of(((a_ref[0] + d) % SIDE) * part, 128) for d in range(SIDE)
    ]
    load = pltpu.make_async_copy(down_ref, down, sems.at[2 * SIDE])
    load.start()
    copies = []
    for d in (1, 3, 2, 0):
        for k, ref in enumerate((gate_ref, up_ref)):
            copy = pltpu.make_async_copy(
                ref.at[pl.ds(starts[d], part), :],
                outs[d].at[:, pl.ds(k * units, units)],
                sems.at[2 * d + k],
            )
            copy.start()
            copies.append(copy)
    load.wait()
    for d, out_ref in enumerate(outs):
        out_ref[:, 2 * units :] = down[:, pl.ds(starts[d], part)].T
    for copy in copies:
        copy.wait()


def pack_weights(a, gate_w, up_w, down_w):
    width, units = gate_w.shape
    return pl.pallas_call(
        pack_kernel,
        in_specs=[SMEM, ANY, ANY, ANY],
        out_shape=[shape(width // SIDE, 3 * units)] * SIDE,
        scratch_shapes=[
            pltpu.VMEM((units, width), BF16),
            pltpu.SemaphoreType.DMA((2 * SIDE + 1,)),
        ],
        compiler_params=PARAMS,
        name="pack_weights",
    )(a, gate_w, up_w, down_w)


def table_kernel(lengths_ref, ids_ref, codes_ref, rows_ref, scale_ref, table_ref):
    experts, tok_count = ids_ref.shape
    folded = 2 * SIDE * CAP
    row_count = experts * folded
    ids = ids_ref[...]
    codes = codes_ref[...]
    slot_len = tok_count // 2
    position = lax.broadcasted_iota(jnp.int32, (1, tok_count), 1)
    bound = jnp.where(position < slot_len, lengths_ref[0, 0], lengths_ref[0, 1] + slot_len)
    live = position < bound
    expert = lax.broadcasted_iota(jnp.int32, (experts, tok_count), 0)
    member = jnp.zeros((experts, tok_count), F32)
    gate = jnp.zeros((experts, tok_count), F32)
    for e in range(experts):
        hit = ids == e
        found = jnp.sum(hit.astype(F32), axis=0, keepdims=True)
        code = jnp.sum(jnp.where(hit, codes, 0).astype(F32), axis=0, keepdims=True)
        here = jnp.logical_and(live, found > 0.0)
        member = jnp.where(jnp.logical_and(expert == e, here), 1.0, member)
        gate = jnp.where(expert == e, code / GRID_SCALE, gate)
    earlier = lax.broadcasted_iota(jnp.int32, (tok_count, tok_count), 0)
    later = lax.broadcasted_iota(jnp.int32, (tok_count, tok_count), 1)
    rank = dot(member.astype(BF16), (earlier < later).astype(BF16), NN)
    slot_of = jnp.where(member > 0.0, rank, -1.0)

    def spread(x, times):
        return jnp.broadcast_to(x[:, None, :], (experts, times, tok_count)).reshape(
            experts * times, tok_count
        )

    row = lax.broadcasted_iota(jnp.int32, (row_count, tok_count), 0)
    chosen = spread(slot_of, folded) == (row % CAP).astype(F32)
    part = (row // CAP) % (2 * SIDE)
    for p in range(2 * SIDE):
        mine = jnp.logical_and(chosen, part == p)
        rows_ref[:, p * tok_count : (p + 1) * tok_count] = mine.astype(BF16)
    weight = jnp.sum(jnp.where(chosen, spread(gate, folded), 0.0), axis=1, keepdims=True)
    is_grad = (part % 2)[:, :1] == 1
    scale_ref[...] = jnp.broadcast_to(jnp.where(is_grad, weight, 1.0), scale_ref.shape)
    row = lax.broadcasted_iota(jnp.int32, table_ref.shape, 0)
    chosen = spread(slot_of, SIDE * CAP) == (row % CAP).astype(F32)
    table_ref[...] = chosen.astype(BF16)


def slot_tables(expert_ids, gate_codes, lengths, experts):
    tok_count = expert_ids.shape[0]
    row_count = experts * 2 * SIDE * CAP
    return pl.pallas_call(
        table_kernel,
        in_specs=[SMEM, VMEM, VMEM],
        out_shape=[
            shape(row_count, 2 * SIDE * tok_count),
            shape(row_count, 128, dtype=F32),
            shape(experts * SIDE * CAP, tok_count),
        ],
        compiler_params=PARAMS,
        name="slot_tables",
    )(lengths, expert_ids.T, gate_codes.T)


def select_kernel(rows_ref, scale_ref, tokens_ref, grads_ref, out_ref):
    tok_count = tokens_ref.shape[0]
    part = out_ref.shape[1]
    total = None
    for q in range(SIDE):
        span = slice(q * part, (q + 1) * part)
        for array, ref in enumerate((tokens_ref, grads_ref)):
            p = 2 * q + array
            term = dot(
                rows_ref[:, p * tok_count : (p + 1) * tok_count], ref[:, span], NN
            )
            total = term if total is None else total + term
    out_ref[...] = (scale_ref[:, :1] * total).astype(BF16)


def select_rows(rows, scale, tokens, grad_out):
    return pl.pallas_call(
        select_kernel,
        in_specs=[VMEM] * 4,
        out_shape=shape(rows.shape[0], tokens.shape[1] // SIDE),
        compiler_params=PARAMS,
        name="select_rows",
    )(rows, scale, tokens, grad_out)


def exchange(x, experts):
    folded, width = x.shape
    blocks = x.reshape(experts, folded // experts, width)
    return lax.all_to_all(
        blocks, ("grp", "sp"), split_axis=0, concat_axis=0, tiled=True
    ).reshape(folded, width)


def unfold_kernel(a_ref, x_ref, *refs):
    out_refs = refs[-SIDE:]
    rows, folded = out_refs[0].shape[0], x_ref.shape[0]
    part = x_ref.shape[1]
    to = lax.broadcasted_iota(jnp.int32, (rows, folded), 0)
    src = lax.broadcasted_iota(jnp.int32, (rows, folded), 1)
    first = (to // CAP) * (2 * SIDE * CAP) + to % CAP
    for d, out_ref in enumerate(out_refs):
        quarter = (a_ref[0] + d) % SIDE
        for array in range(2):
            pick = (src == first + (quarter * 2 + array) * CAP).astype(BF16)
            out_ref[:, array * part : (array + 1) * part] = dot(
                pick, x_ref[...], NN
            ).astype(BF16)


def unfold(a, x, after):
    folded, part = x.shape
    rows = folded // (2 * SIDE)
    return pl.pallas_call(
        unfold_kernel,
        in_specs=[SMEM, VMEM] + [ANY] * len(after),
        out_shape=[shape(rows, 2 * part)] * SIDE,
        compiler_params=PARAMS,
        name="unfold",
    )(a, x, *after)


def line_kernel(a_ref, *refs):
    halves = refs[-2:]
    for d, x_ref in enumerate(refs[:SIDE]):
        rows = x_ref.shape[0]
        place = (a_ref[0] + SIDE - d) % SIDE
        at = pl.multiple_of((place % 2) * rows, 16)
        for h, out_ref in enumerate(halves):

            @pl.when(place // 2 == h)
            def _(x_ref=x_ref, out_ref=out_ref, at=at, rows=rows):
                out_ref[pl.ds(at, rows), :] = x_ref[...]


def line_up(a, blocks):
    rows, width = blocks[0].shape
    return pl.pallas_call(
        line_kernel,
        in_specs=[SMEM] + [VMEM] * SIDE,
        out_shape=[shape(SIDE // 2 * rows, width)] * 2,
        compiler_params=PARAMS,
        name="line_up",
    )(a, *blocks)


def join_kernel(first_ref, second_ref, third_ref, fourth_ref, up_ref, down_ref):
    half = first_ref.shape[0]
    up_ref[:half, :] = first_ref[...]
    up_ref[half:, :] = second_ref[...]
    down_ref[:half, :] = third_ref[...]
    down_ref[half:, :] = fourth_ref[...]


def join(*halves):
    rows, width = halves[0].shape
    return pl.pallas_call(
        join_kernel,
        in_specs=[VMEM] * 4,
        out_shape=[shape(2 * rows, width)] * 2,
        compiler_params=PARAMS,
        name="join",
    )(*halves)


def forward_kernel(count, *refs):
    pieces, weights, outs = refs[:count], refs[count : count + SIDE], refs[-SIDE:]
    part = weights[0].shape[0]
    units = weights[0].shape[1] // 3
    at = 0
    for piece in pieces:
        span = slice(at, at + piece.shape[0])
        at += piece.shape[0]
        for weight, out in zip(weights, outs):
            inner = dot(piece[:, :part], weight[:, : 2 * units], NN)
            out[span, : 2 * units] = inner.astype(out.dtype)
            outer = dot(piece[:, part:], weight[:, 2 * units :], NN)
            out[span, 2 * units :] = outer.astype(out.dtype)


def forward(pieces, weights, after):
    rows = sum(piece.shape[0] for piece in pieces)
    part, columns = weights[0].shape
    return pl.pallas_call(
        functools.partial(forward_kernel, len(pieces)),
        in_specs=[VMEM] * (len(pieces) + SIDE) + [ANY] * len(after),
        out_shape=[shape(rows, columns, dtype=F32)] + [shape(rows, columns)] * (SIDE - 1),
        compiler_params=PARAMS,
        cost_estimate=pl.CostEstimate(
            flops=2 * SIDE * rows * part * columns,
            bytes_accessed=4 * rows * part + 2 * SIDE * (part + rows) * columns,
            transcendentals=0,
        ),
        name="forward",
    )(*pieces, *weights, *after)


def activate_kernel(*refs):
    out_ref = refs[-1]
    units = out_ref.shape[1] // 3
    at = 0
    for g in range(0, len(refs) - 1, SIDE):
        total = refs[g][...]
        for term in refs[g + 1 : g + SIDE]:
            total = total + term[...].astype(F32)
        span = slice(at, at + total.shape[0])
        at += total.shape[0]
        gate_pre, up_pre, hidden_grad = (
            total[:, :units], total[:, units : 2 * units], total[:, 2 * units :],
        )
        logistic = 1.0 / (1.0 + jnp.exp(-gate_pre))
        out_ref[span, :units] = (gate_pre * logistic * up_pre).astype(BF16)
        out_ref[span, units : 2 * units] = (
            hidden_grad * up_pre * logistic * (1.0 + gate_pre * (1.0 - logistic))
        ).astype(BF16)
        out_ref[span, 2 * units :] = (hidden_grad * gate_pre * logistic).astype(BF16)


def activate(groups):
    rows = sum(terms[0].shape[0] for terms in groups)
    return pl.pallas_call(
        activate_kernel,
        in_specs=[VMEM] * (SIDE * len(groups)),
        out_shape=shape(rows, groups[0][0].shape[1]),
        compiler_params=PARAMS,
        name="activate",
    )(*[term for terms in groups for term in terms])


def backward_kernel(blocks, *refs):
    chunks = (refs[:SIDE], refs[SIDE : 2 * SIDE])
    weights, outs = refs[2 * SIDE : 3 * SIDE], refs[-len(blocks) :]
    units = weights[0].shape[1] // 3
    for block, out in zip(blocks, outs):
        rows = out.shape[0] // 2
        for k, half in enumerate(block):
            at = half % SIDE * rows
            total = None
            for h, weight in zip(chunks[half // SIDE], weights):
                term = dot(h[at : at + rows, units:], weight[:, : 2 * units], NT)
                total = term if total is None else total + term
            out[k * rows : (k + 1) * rows, :] = total.astype(out.dtype)


def backward(hidden, weights, blocks, dtype, after):
    rows = hidden[0][0].shape[0] // 2
    part, columns = weights[0].shape
    return pl.pallas_call(
        functools.partial(backward_kernel, blocks),
        in_specs=[VMEM] * (3 * SIDE) + [ANY] * len(after),
        out_shape=[shape(rows, part, dtype=dtype) for _ in blocks],
        compiler_params=PARAMS,
        cost_estimate=pl.CostEstimate(
            flops=2 * SIDE * rows * len(blocks) * part * columns * 2 // 3,
            bytes_accessed=2 * SIDE * (part + rows * len(blocks)) * columns,
            transcendentals=0,
        ),
        name="backward",
    )(*hidden[0], *hidden[1], *weights, *after)


def weight_kernel(layout, *refs):
    count = sum(layout)
    pieces, chunks, out_ref = refs[:count], refs[count : count + len(layout)], refs[-1]
    units = out_ref.shape[1]
    part = out_ref.shape[0] // 3
    inner, outer, i = None, None, 0
    for hidden, members in zip(chunks, layout):
        at = 0
        for piece in pieces[i : i + members]:
            span = slice(at, at + piece.shape[0])
            at += piece.shape[0]
            term = dot(piece[:, :part], hidden[span, units:], TN)
            inner = term if inner is None else inner + term
            term = dot(hidden[span, :units], piece[:, part:], TN)
            outer = term if outer is None else outer + term
        i += members
    out_ref[:part, :] = inner[:, :units].astype(BF16)
    out_ref[part : 2 * part, :] = inner[:, units:].astype(BF16)
    for k in range(part // units):
        out_ref[2 * part + k * units : 2 * part + (k + 1) * units, :] = outer[
            :, k * units : (k + 1) * units
        ].astype(BF16)


def weight_grads(groups, hidden, after):
    pieces = [piece for group in groups for piece in group]
    part = pieces[0].shape[1] // 2
    columns = hidden[0].shape[1]
    rows = sum(h.shape[0] for h in hidden)
    return pl.pallas_call(
        functools.partial(weight_kernel, tuple(len(group) for group in groups)),
        in_specs=[VMEM] * (len(pieces) + len(hidden)) + [ANY] * len(after),
        out_shape=shape(3 * part, columns // 3),
        compiler_params=PARAMS,
        cost_estimate=pl.CostEstimate(
            flops=2 * rows * part * columns,
            bytes_accessed=4 * rows * part + 2 * (part + rows) * columns,
            transcendentals=0,
        ),
        name="weight_grads",
    )(*pieces, *hidden, *after)


def unpack_kernel(steps, a_ref, *refs):
    count = len(steps)
    gate_ref, up_ref, down_ref, mark_ref, sems = refs[-5:]
    units = gate_ref.shape[1]
    part = gate_ref.shape[0] // SIDE
    copies = []
    for i, (step, x_ref) in enumerate(zip(steps, refs[:count])):
        quarter = (a_ref[0] + step) % SIDE
        at = pl.multiple_of(quarter * part, 128)
        pairs = [
            (x_ref.at[pl.ds(0, part), :], gate_ref.at[pl.ds(at, part), :]),
            (x_ref.at[pl.ds(part, part), :], up_ref.at[pl.ds(at, part), :]),
        ]
        for k in range(part // units):
            pairs.append(
                (
                    x_ref.at[pl.ds(2 * part + k * units, units), :],
                    down_ref.at[:, pl.ds(pl.multiple_of(at + k * units, 128), units)],
                )
            )
        for k, (source, target) in enumerate(pairs):
            copy = pltpu.make_async_copy(source, target, sems.at[i, k])
            copy.start()
            copies.append(copy)
    mark_ref[...] = jnp.zeros_like(mark_ref)
    for copy in copies:
        copy.wait()


def unpack(a, steps, arrays, into):
    rows, units = arrays[0].shape
    part = rows // 3
    width = part * SIDE
    earlier = [] if into is None else list(into)
    return pl.pallas_call(
        functools.partial(unpack_kernel, steps),
        in_specs=[SMEM] + [ANY] * (len(arrays) + len(earlier)),
        out_specs=[ANY, ANY, ANY, VMEM],
        out_shape=[
            shape(width, units),
            shape(width, units),
            shape(units, width),
            shape(8, 128, dtype=F32),
        ],
        scratch_shapes=[pltpu.SemaphoreType.DMA((len(arrays), 2 + part // units))],
        input_output_aliases={1 + len(arrays) + i: i for i in range(len(earlier))},
        compiler_params=PARAMS,
        name="unpack",
    )(a, *arrays, *earlier)


def sum_kernel(a_ref, *refs):
    terms, outs = refs[:SIDE], refs[-SIDE:]
    rows = outs[0].shape[0]
    for d, out in enumerate(outs):
        at = pl.multiple_of(((a_ref[0] + d) % SIDE) * rows, 16)
        total = None
        for term in terms:
            x = term[pl.ds(at, rows), :].astype(F32)
            total = x if total is None else total + x
        out[...] = total.astype(BF16)


def sum_rows(a, terms, after):
    rows, part = terms[0].shape
    return pl.pallas_call(
        sum_kernel,
        in_specs=[SMEM] + [VMEM] * SIDE + [ANY] * len(after),
        out_shape=[shape(rows // SIDE, part)] * SIDE,
        compiler_params=PARAMS,
        name="sum_rows",
    )(a, *terms, *after)


def fold_kernel(a_ref, *refs):
    out_ref = refs[-1]
    folded, rows = out_ref.shape[0], refs[0].shape[0]
    to = lax.broadcasted_iota(jnp.int32, (folded, rows), 0)
    src = lax.broadcasted_iota(jnp.int32, (folded, rows), 1)
    first = (src // CAP) * (SIDE * CAP) + src % CAP
    total = None
    for d, x_ref in enumerate(refs[:SIDE]):
        quarter = (a_ref[0] + SIDE - d) % SIDE
        term = dot((to == first + quarter * CAP).astype(BF16), x_ref[...], NN)
        total = term if total is None else total + term
    out_ref[...] = total.astype(BF16)


def fold(a, blocks):
    rows, part = blocks[0].shape
    return pl.pallas_call(
        fold_kernel,
        in_specs=[SMEM] + [VMEM] * SIDE,
        out_shape=shape(rows * SIDE, part),
        compiler_params=PARAMS,
        name="fold",
    )(a, *blocks)


def hold_kernel(*refs):
    pass


def hold(arrays, after):
    return pl.pallas_call(
        hold_kernel,
        in_specs=[ANY] * (len(arrays) + len(after)),
        out_specs=[ANY] * len(arrays),
        out_shape=[shape(*x.shape) for x in arrays],
        input_output_aliases={i: i for i in range(len(arrays))},
        compiler_params=PARAMS,
        name="hold",
    )(*arrays, *after)


def combine_kernel(table_ref, x_ref, out_ref, held_ref, sems):
    table = table_ref[...]
    row = lax.broadcasted_iota(jnp.int32, table.shape, 0)
    part = x_ref.shape[1]
    copies = []
    for q in range(SIDE):
        mine = jnp.where((row // CAP) % SIDE == q, table, jnp.zeros_like(table))
        span = pl.ds(q * part, part)
        held_ref[:, span] = dot(mine, x_ref[...], TN).astype(BF16)
        copy = pltpu.make_async_copy(
            held_ref.at[:, span], out_ref.at[:, span], sems.at[q]
        )
        copy.start()
        copies.append(copy)
    for copy in copies:
        copy.wait()


def combine(table, x):
    part = x.shape[1]
    tok_count = table.shape[1]
    return pl.pallas_call(
        combine_kernel,
        in_specs=[VMEM, VMEM],
        out_specs=ANY,
        out_shape=shape(tok_count, part * SIDE),
        scratch_shapes=[
            pltpu.VMEM((tok_count, part * SIDE), BF16),
            pltpu.SemaphoreType.DMA((SIDE,)),
        ],
        compiler_params=PARAMS,
        name="combine",
    )(table, x)


def body(tokens, grad_out, expert_ids, gate_codes, lengths, w_gate, w_up, w_down):
    experts = lax.axis_size("grp") * lax.axis_size("sp")
    dp = lax.axis_index("dp")
    a = jnp.where(lax.axis_index("grp") == 0, dp % SIDE, dp // SIDE).astype(jnp.int32)[None]
    gate_w, up_w, down_w = w_gate[0], w_up[0], w_down[0]

    rows, scale, table = slot_tables(expert_ids, gate_codes, lengths, experts)
    sent = select_rows(rows, scale, tokens, grad_out)
    packed = pack_weights(a, gate_w, up_w, down_w)
    weights = [packed[0]] + [shift(packed[d], True, d) for d in range(1, SIDE)]

    blocks = unfold(a, exchange(sent, experts), weights[1:])
    blocks = [blocks[0]] + [shift(blocks[d], True, d) for d in range(1, SIDE)]
    head, tail = line_up(a, blocks)
    after_head, before_tail = shift(head, False, 1), shift(tail, False, -1)
    up, down = join(after_head, tail, before_tail, head)
    early = [head, tail, after_head, before_tail]
    late = [shift(up, False, 1), shift(down, False, -1)]

    def presums(pieces, after):
        terms = forward(pieces, weights, after)
        return [terms[0]] + [shift(terms[d], True, -d) for d in range(1, SIDE)]

    def spread(acts):
        return [acts] + [shift(acts, True, d) for d in range(1, SIDE)]

    most = presums(early, [])
    rest = presums(late, [most[0]])
    hidden = [spread(activate([most])), spread(activate([rest]))]
    groups = [early, late]

    own_rows, before_rows, after_rows, far_rows = (0, 1), (2, 5), (7, 3), (4, 6)

    def grads_of(d, after):
        return weight_grads(groups, [chunk[d] for chunk in hidden], after)

    across = grads_of(2, [chunk[d] for chunk in hidden for d in (1, 3)])
    (to_far,) = backward(hidden, weights, (far_rows,), BF16, [across])
    to_before, to_after = backward(
        hidden, weights, (before_rows, after_rows), BF16, [to_far]
    )
    (own,) = backward(hidden, weights, (own_rows,), F32, [to_after])
    row_terms = [
        own,
        shift(to_before, False, -1),
        shift(to_after, False, 1),
        shift(to_far, False, 2),
    ]
    *into, mark = unpack(a, (0,), [grads_of(0, [own])], None)
    grads = [grads_of(d, [own]) for d in (1, 3)]
    *into, mark = unpack(a, (2,), [shift(across, True, -2)], into)
    parts = sum_rows(a, row_terms, [mark] + grads)
    returned = [parts[0]] + [shift(parts[d], True, d) for d in range(1, SIDE)]
    grads = hold(grads, returned[1:])
    folded = fold(a, returned)
    grads = [shift(x, True, -d) for d, x in zip((1, 3), grads)]
    grad_tokens = combine(table, exchange(folded, experts))
    *into, _ = unpack(a, (1, 3), grads, into)
    gate_w_grad, up_w_grad, down_w_grad = into
    return (grad_tokens, gate_w_grad[None], up_w_grad[None], down_w_grad[None])


def solution(mesh):
    return jax.shard_map(
        body,
        mesh=mesh,
        in_specs=(
            P(("grp", "dp", "sp"), None),
            P(("grp", "dp", "sp"), None),
            P(("grp", "dp", "sp"), None),
            P(("grp", "dp", "sp"), None),
            P(("grp", "dp", "sp"), None),
            P(("grp", "sp"), None, "dp"),
            P(("grp", "sp"), None, "dp"),
            P(("grp", "sp"), "dp", None),
        ),
        out_specs=(
            P(("grp", "dp", "sp"), None),
            P(("grp", "sp"), None, "dp"),
            P(("grp", "sp"), None, "dp"),
            P(("grp", "sp"), "dp", None),
        ),
        check_vma=False,
    )
```

```python
import functools

import jax
import jax.numpy as jnp
from jax import lax
from jax.experimental import pallas as pl
from jax.experimental.pallas import tpu as pltpu
from jax.sharding import PartitionSpec as P

CAP = 6
SIDE = 4
GRID_SCALE = 2048.0
BF16 = jnp.bfloat16
F32 = jnp.float32
MIB = 1024 * 1024
PARAMS = pltpu.CompilerParams(vmem_limit_bytes=24 * MIB)
SMEM = pl.BlockSpec(memory_space=pltpu.SMEM)
VMEM = pl.BlockSpec(memory_space=pltpu.VMEM)
ANY = pl.BlockSpec(memory_space=pl.ANY)


def dot(a, b, contract):
    return lax.dot_general(a, b, (contract, ((), ())), preferred_element_type=F32)


NN = ((1,), (0,))
NT = ((1,), (1,))
TN = ((0,), (0,))


def shape(*dims, dtype=BF16):
    return jax.ShapeDtypeStruct(dims, dtype)


def shift(x, along_a, step):
    pairs = []
    for grp in range(2):
        for y in range(SIDE):
            for z in range(SIDE):
                if (grp == 0) == along_a:
                    to = (y, (z + step) % SIDE)
                else:
                    to = ((y + step) % SIDE, z)
                pairs.append(
                    (grp * SIDE * SIDE + y * SIDE + z, grp * SIDE * SIDE + to[0] * SIDE + to[1])
                )
    return lax.ppermute(x, ("grp", "dp"), pairs)


def pack_kernel(a_ref, gate_ref, up_ref, down_ref, *refs):
    outs, down, sems = refs[:SIDE], refs[SIDE], refs[SIDE + 1]
    part, units = outs[0].shape[0], down.shape[0]
    starts = [
        pl.multiple_of(((a_ref[0] + d) % SIDE) * part, 128) for d in range(SIDE)
    ]
    load = pltpu.make_async_copy(down_ref, down, sems.at[2 * SIDE])
    load.start()
    copies = []
    for d in (1, 3, 2, 0):
        for k, ref in enumerate((gate_ref, up_ref)):
            copy = pltpu.make_async_copy(
                ref.at[pl.ds(starts[d], part), :],
                outs[d].at[:, pl.ds(k * units, units)],
                sems.at[2 * d + k],
            )
            copy.start()
            copies.append(copy)
    load.wait()
    for d, out_ref in enumerate(outs):
        out_ref[:, 2 * units :] = down[:, pl.ds(starts[d], part)].T
    for copy in copies:
        copy.wait()


def pack_weights(a, gate_w, up_w, down_w):
    width, units = gate_w.shape
    return pl.pallas_call(
        pack_kernel,
        in_specs=[SMEM, ANY, ANY, ANY],
        out_shape=[shape(width // SIDE, 3 * units)] * SIDE,
        scratch_shapes=[
            pltpu.VMEM((units, width), BF16),
            pltpu.SemaphoreType.DMA((2 * SIDE + 1,)),
        ],
        compiler_params=PARAMS,
        name="pack_weights",
    )(a, gate_w, up_w, down_w)


def table_kernel(lengths_ref, ids_ref, codes_ref, rows_ref, scale_ref, table_ref):
    experts, tok_count = ids_ref.shape
    folded = 2 * SIDE * CAP
    row_count = experts * folded
    ids = ids_ref[...]
    codes = codes_ref[...]
    slot_len = tok_count // 2
    position = lax.broadcasted_iota(jnp.int32, (1, tok_count), 1)
    bound = jnp.where(position < slot_len, lengths_ref[0, 0], lengths_ref[0, 1] + slot_len)
    live = position < bound
    expert = lax.broadcasted_iota(jnp.int32, (experts, tok_count), 0)
    member = jnp.zeros((experts, tok_count), F32)
    gate = jnp.zeros((experts, tok_count), F32)
    for e in range(experts):
        hit = ids == e
        found = jnp.sum(hit.astype(F32), axis=0, keepdims=True)
        code = jnp.sum(jnp.where(hit, codes, 0).astype(F32), axis=0, keepdims=True)
        here = jnp.logical_and(live, found > 0.0)
        member = jnp.where(jnp.logical_and(expert == e, here), 1.0, member)
        gate = jnp.where(expert == e, code / GRID_SCALE, gate)
    earlier = lax.broadcasted_iota(jnp.int32, (tok_count, tok_count), 0)
    later = lax.broadcasted_iota(jnp.int32, (tok_count, tok_count), 1)
    rank = dot(member.astype(BF16), (earlier < later).astype(BF16), NN)
    slot_of = jnp.where(member > 0.0, rank, -1.0)

    def spread(x, times):
        return jnp.broadcast_to(x[:, None, :], (experts, times, tok_count)).reshape(
            experts * times, tok_count
        )

    row = lax.broadcasted_iota(jnp.int32, (row_count, tok_count), 0)
    chosen = spread(slot_of, folded) == (row % CAP).astype(F32)
    part = (row // CAP) % (2 * SIDE)
    for p in range(2 * SIDE):
        mine = jnp.logical_and(chosen, part == p)
        rows_ref[:, p * tok_count : (p + 1) * tok_count] = mine.astype(BF16)
    weight = jnp.sum(jnp.where(chosen, spread(gate, folded), 0.0), axis=1, keepdims=True)
    is_grad = (part % 2)[:, :1] == 1
    scale_ref[...] = jnp.broadcast_to(jnp.where(is_grad, weight, 1.0), scale_ref.shape)
    row = lax.broadcasted_iota(jnp.int32, table_ref.shape, 0)
    chosen = spread(slot_of, SIDE * CAP) == (row % CAP).astype(F32)
    table_ref[...] = chosen.astype(BF16)


def slot_tables(expert_ids, gate_codes, lengths, experts):
    tok_count = expert_ids.shape[0]
    row_count = experts * 2 * SIDE * CAP
    return pl.pallas_call(
        table_kernel,
        in_specs=[SMEM, VMEM, VMEM],
        out_shape=[
            shape(row_count, 2 * SIDE * tok_count),
            shape(row_count, 128, dtype=F32),
            shape(experts * SIDE * CAP, tok_count),
        ],
        compiler_params=PARAMS,
        name="slot_tables",
    )(lengths, expert_ids.T, gate_codes.T)


def select_kernel(rows_ref, scale_ref, tokens_ref, grads_ref, out_ref):
    tok_count = tokens_ref.shape[0]
    part = out_ref.shape[1]
    total = None
    for q in range(SIDE):
        span = slice(q * part, (q + 1) * part)
        for array, ref in enumerate((tokens_ref, grads_ref)):
            p = 2 * q + array
            term = dot(
                rows_ref[:, p * tok_count : (p + 1) * tok_count], ref[:, span], NN
            )
            total = term if total is None else total + term
    out_ref[...] = (scale_ref[:, :1] * total).astype(BF16)


def select_rows(rows, scale, tokens, grad_out):
    return pl.pallas_call(
        select_kernel,
        in_specs=[VMEM] * 4,
        out_shape=shape(rows.shape[0], tokens.shape[1] // SIDE),
        compiler_params=PARAMS,
        name="select_rows",
    )(rows, scale, tokens, grad_out)


def exchange(x, experts):
    folded, width = x.shape
    blocks = x.reshape(experts, folded // experts, width)
    return lax.all_to_all(
        blocks, ("grp", "sp"), split_axis=0, concat_axis=0, tiled=True
    ).reshape(folded, width)


def unfold_kernel(a_ref, x_ref, *refs):
    out_refs = refs[-SIDE:]
    rows, folded = out_refs[0].shape[0], x_ref.shape[0]
    part = x_ref.shape[1]
    to = lax.broadcasted_iota(jnp.int32, (rows, folded), 0)
    src = lax.broadcasted_iota(jnp.int32, (rows, folded), 1)
    first = (to // CAP) * (2 * SIDE * CAP) + to % CAP
    for d, out_ref in enumerate(out_refs):
        quarter = (a_ref[0] + d) % SIDE
        for array in range(2):
            pick = (src == first + (quarter * 2 + array) * CAP).astype(BF16)
            out_ref[:, array * part : (array + 1) * part] = dot(
                pick, x_ref[...], NN
            ).astype(BF16)


def unfold(a, x, after):
    folded, part = x.shape
    rows = folded // (2 * SIDE)
    return pl.pallas_call(
        unfold_kernel,
        in_specs=[SMEM, VMEM] + [ANY] * len(after),
        out_shape=[shape(rows, 2 * part)] * SIDE,
        compiler_params=PARAMS,
        name="unfold",
    )(a, x, *after)


def line_kernel(a_ref, *refs):
    halves = refs[-2:]
    for d, x_ref in enumerate(refs[:SIDE]):
        rows = x_ref.shape[0]
        place = (a_ref[0] + SIDE - d) % SIDE
        at = pl.multiple_of((place % 2) * rows, 16)
        for h, out_ref in enumerate(halves):

            @pl.when(place // 2 == h)
            def _(x_ref=x_ref, out_ref=out_ref, at=at, rows=rows):
                out_ref[pl.ds(at, rows), :] = x_ref[...]


def line_up(a, blocks):
    rows, width = blocks[0].shape
    return pl.pallas_call(
        line_kernel,
        in_specs=[SMEM] + [VMEM] * SIDE,
        out_shape=[shape(SIDE // 2 * rows, width)] * 2,
        compiler_params=PARAMS,
        name="line_up",
    )(a, *blocks)


def join_kernel(first_ref, second_ref, third_ref, fourth_ref, up_ref, down_ref):
    half = first_ref.shape[0]
    up_ref[:half, :] = first_ref[...]
    up_ref[half:, :] = second_ref[...]
    down_ref[:half, :] = third_ref[...]
    down_ref[half:, :] = fourth_ref[...]


def join(*halves):
    rows, width = halves[0].shape
    return pl.pallas_call(
        join_kernel,
        in_specs=[VMEM] * 4,
        out_shape=[shape(2 * rows, width)] * 2,
        compiler_params=PARAMS,
        name="join",
    )(*halves)


def forward_kernel(count, *refs):
    pieces, weights, outs = refs[:count], refs[count : count + SIDE], refs[-SIDE:]
    part = weights[0].shape[0]
    units = weights[0].shape[1] // 3
    at = 0
    for piece in pieces:
        span = slice(at, at + piece.shape[0])
        at += piece.shape[0]
        for weight, out in zip(weights, outs):
            inner = dot(piece[:, :part], weight[:, : 2 * units], NN)
            out[span, : 2 * units] = inner.astype(out.dtype)
            outer = dot(piece[:, part:], weight[:, 2 * units :], NN)
            out[span, 2 * units :] = outer.astype(out.dtype)


def forward(pieces, weights, after):
    rows = sum(piece.shape[0] for piece in pieces)
    part, columns = weights[0].shape
    return pl.pallas_call(
        functools.partial(forward_kernel, len(pieces)),
        in_specs=[VMEM] * (len(pieces) + SIDE) + [ANY] * len(after),
        out_shape=[shape(rows, columns, dtype=F32)] + [shape(rows, columns)] * (SIDE - 1),
        compiler_params=PARAMS,
        cost_estimate=pl.CostEstimate(
            flops=2 * SIDE * rows * part * columns,
            bytes_accessed=4 * rows * part + 2 * SIDE * (part + rows) * columns,
            transcendentals=0,
        ),
        name="forward",
    )(*pieces, *weights, *after)


def activate_kernel(*refs):
    out_ref = refs[-1]
    units = out_ref.shape[1] // 3
    at = 0
    for g in range(0, len(refs) - 1, SIDE):
        total = refs[g][...]
        for term in refs[g + 1 : g + SIDE]:
            total = total + term[...].astype(F32)
        span = slice(at, at + total.shape[0])
        at += total.shape[0]
        gate_pre, up_pre, hidden_grad = (
            total[:, :units], total[:, units : 2 * units], total[:, 2 * units :],
        )
        logistic = 1.0 / (1.0 + jnp.exp(-gate_pre))
        out_ref[span, :units] = (gate_pre * logistic * up_pre).astype(BF16)
        out_ref[span, units : 2 * units] = (
            hidden_grad * up_pre * logistic * (1.0 + gate_pre * (1.0 - logistic))
        ).astype(BF16)
        out_ref[span, 2 * units :] = (hidden_grad * gate_pre * logistic).astype(BF16)


def activate(groups):
    rows = sum(terms[0].shape[0] for terms in groups)
    return pl.pallas_call(
        activate_kernel,
        in_specs=[VMEM] * (SIDE * len(groups)),
        out_shape=shape(rows, groups[0][0].shape[1]),
        compiler_params=PARAMS,
        name="activate",
    )(*[term for terms in groups for term in terms])


def backward_kernel(blocks, *refs):
    chunks = (refs[:SIDE], refs[SIDE : 2 * SIDE])
    weights, outs = refs[2 * SIDE : 3 * SIDE], refs[-len(blocks) :]
    units = weights[0].shape[1] // 3
    for block, out in zip(blocks, outs):
        rows = out.shape[0] // 2
        for k, half in enumerate(block):
            at = half % SIDE * rows
            total = None
            for h, weight in zip(chunks[half // SIDE], weights):
                term = dot(h[at : at + rows, units:], weight[:, : 2 * units], NT)
                total = term if total is None else total + term
            out[k * rows : (k + 1) * rows, :] = total.astype(out.dtype)


def backward(hidden, weights, blocks, dtype, after):
    rows = hidden[0][0].shape[0] // 2
    part, columns = weights[0].shape
    return pl.pallas_call(
        functools.partial(backward_kernel, blocks),
        in_specs=[VMEM] * (3 * SIDE) + [ANY] * len(after),
        out_shape=[shape(rows, part, dtype=dtype) for _ in blocks],
        compiler_params=PARAMS,
        cost_estimate=pl.CostEstimate(
            flops=2 * SIDE * rows * len(blocks) * part * columns * 2 // 3,
            bytes_accessed=2 * SIDE * (part + rows * len(blocks)) * columns,
            transcendentals=0,
        ),
        name="backward",
    )(*hidden[0], *hidden[1], *weights, *after)


def weight_kernel(layout, *refs):
    count = sum(layout)
    pieces, chunks, out_ref = refs[:count], refs[count : count + len(layout)], refs[-1]
    units = out_ref.shape[1]
    part = out_ref.shape[0] // 3
    inner, outer, i = None, None, 0
    for hidden, members in zip(chunks, layout):
        at = 0
        for piece in pieces[i : i + members]:
            span = slice(at, at + piece.shape[0])
            at += piece.shape[0]
            term = dot(piece[:, :part], hidden[span, units:], TN)
            inner = term if inner is None else inner + term
            term = dot(hidden[span, :units], piece[:, part:], TN)
            outer = term if outer is None else outer + term
        i += members
    out_ref[:part, :] = inner[:, :units].astype(BF16)
    out_ref[part : 2 * part, :] = inner[:, units:].astype(BF16)
    for k in range(part // units):
        out_ref[2 * part + k * units : 2 * part + (k + 1) * units, :] = outer[
            :, k * units : (k + 1) * units
        ].astype(BF16)


def weight_grads(groups, hidden, after):
    pieces = [piece for group in groups for piece in group]
    part = pieces[0].shape[1] // 2
    columns = hidden[0].shape[1]
    rows = sum(h.shape[0] for h in hidden)
    return pl.pallas_call(
        functools.partial(weight_kernel, tuple(len(group) for group in groups)),
        in_specs=[VMEM] * (len(pieces) + len(hidden)) + [ANY] * len(after),
        out_shape=shape(3 * part, columns // 3),
        compiler_params=PARAMS,
        cost_estimate=pl.CostEstimate(
            flops=2 * rows * part * columns,
            bytes_accessed=4 * rows * part + 2 * (part + rows) * columns,
            transcendentals=0,
        ),
        name="weight_grads",
    )(*pieces, *hidden, *after)


def unpack_kernel(steps, a_ref, *refs):
    count = len(steps)
    gate_ref, up_ref, down_ref, mark_ref, sems = refs[-5:]
    units = gate_ref.shape[1]
    part = gate_ref.shape[0] // SIDE
    copies = []
    for i, (step, x_ref) in enumerate(zip(steps, refs[:count])):
        quarter = (a_ref[0] + step) % SIDE
        at = pl.multiple_of(quarter * part, 128)
        pairs = [
            (x_ref.at[pl.ds(0, part), :], gate_ref.at[pl.ds(at, part), :]),
            (x_ref.at[pl.ds(part, part), :], up_ref.at[pl.ds(at, part), :]),
        ]
        for k in range(part // units):
            pairs.append(
                (
                    x_ref.at[pl.ds(2 * part + k * units, units), :],
                    down_ref.at[:, pl.ds(pl.multiple_of(at + k * units, 128), units)],
                )
            )
        for k, (source, target) in enumerate(pairs):
            copy = pltpu.make_async_copy(source, target, sems.at[i, k])
            copy.start()
            copies.append(copy)
    mark_ref[...] = jnp.zeros_like(mark_ref)
    for copy in copies:
        copy.wait()


def unpack(a, steps, arrays, into):
    rows, units = arrays[0].shape
    part = rows // 3
    width = part * SIDE
    earlier = [] if into is None else list(into)
    return pl.pallas_call(
        functools.partial(unpack_kernel, steps),
        in_specs=[SMEM] + [ANY] * (len(arrays) + len(earlier)),
        out_specs=[ANY, ANY, ANY, VMEM],
        out_shape=[
            shape(width, units),
            shape(width, units),
            shape(units, width),
            shape(8, 128, dtype=F32),
        ],
        scratch_shapes=[pltpu.SemaphoreType.DMA((len(arrays), 2 + part // units))],
        input_output_aliases={1 + len(arrays) + i: i for i in range(len(earlier))},
        compiler_params=PARAMS,
        name="unpack",
    )(a, *arrays, *earlier)


def sum_kernel(a_ref, *refs):
    terms, outs = refs[:SIDE], refs[-SIDE:]
    rows = outs[0].shape[0]
    for d, out in enumerate(outs):
        at = pl.multiple_of(((a_ref[0] + d) % SIDE) * rows, 16)
        total = None
        for term in terms:
            x = term[pl.ds(at, rows), :].astype(F32)
            total = x if total is None else total + x
        out[...] = total.astype(BF16)


def sum_rows(a, terms, after):
    rows, part = terms[0].shape
    return pl.pallas_call(
        sum_kernel,
        in_specs=[SMEM] + [VMEM] * SIDE + [ANY] * len(after),
        out_shape=[shape(rows // SIDE, part)] * SIDE,
        compiler_params=PARAMS,
        name="sum_rows",
    )(a, *terms, *after)


def fold_kernel(a_ref, *refs):
    out_ref = refs[-1]
    folded, rows = out_ref.shape[0], refs[0].shape[0]
    to = lax.broadcasted_iota(jnp.int32, (folded, rows), 0)
    src = lax.broadcasted_iota(jnp.int32, (folded, rows), 1)
    first = (src // CAP) * (SIDE * CAP) + src % CAP
    total = None
    for d, x_ref in enumerate(refs[:SIDE]):
        quarter = (a_ref[0] + SIDE - d) % SIDE
        term = dot((to == first + quarter * CAP).astype(BF16), x_ref[...], NN)
        total = term if total is None else total + term
    out_ref[...] = total.astype(BF16)


def fold(a, blocks):
    rows, part = blocks[0].shape
    return pl.pallas_call(
        fold_kernel,
        in_specs=[SMEM] + [VMEM] * SIDE,
        out_shape=shape(rows * SIDE, part),
        compiler_params=PARAMS,
        name="fold",
    )(a, *blocks)


def hold_kernel(*refs):
    pass


def hold(arrays, after):
    return pl.pallas_call(
        hold_kernel,
        in_specs=[ANY] * (len(arrays) + len(after)),
        out_specs=[ANY] * len(arrays),
        out_shape=[shape(*x.shape) for x in arrays],
        input_output_aliases={i: i for i in range(len(arrays))},
        compiler_params=PARAMS,
        name="hold",
    )(*arrays, *after)


def combine_kernel(table_ref, x_ref, out_ref, held_ref, sems):
    table = table_ref[...]
    row = lax.broadcasted_iota(jnp.int32, table.shape, 0)
    part = x_ref.shape[1]
    copies = []
    for q in range(SIDE):
        mine = jnp.where((row // CAP) % SIDE == q, table, jnp.zeros_like(table))
        span = pl.ds(q * part, part)
        held_ref[:, span] = dot(mine, x_ref[...], TN).astype(BF16)
        copy = pltpu.make_async_copy(
            held_ref.at[:, span], out_ref.at[:, span], sems.at[q]
        )
        copy.start()
        copies.append(copy)
    for copy in copies:
        copy.wait()


def combine(table, x):
    part = x.shape[1]
    tok_count = table.shape[1]
    return pl.pallas_call(
        combine_kernel,
        in_specs=[VMEM, VMEM],
        out_specs=ANY,
        out_shape=shape(tok_count, part * SIDE),
        scratch_shapes=[
            pltpu.VMEM((tok_count, part * SIDE), BF16),
            pltpu.SemaphoreType.DMA((SIDE,)),
        ],
        compiler_params=PARAMS,
        name="combine",
    )(table, x)


def body(tokens, grad_out, expert_ids, gate_codes, lengths, w_gate, w_up, w_down):
    experts = lax.axis_size("grp") * lax.axis_size("sp")
    dp = lax.axis_index("dp")
    a = jnp.where(lax.axis_index("grp") == 0, dp % SIDE, dp // SIDE).astype(jnp.int32)[None]
    gate_w, up_w, down_w = w_gate[0], w_up[0], w_down[0]

    rows, scale, table = slot_tables(expert_ids, gate_codes, lengths, experts)
    sent = select_rows(rows, scale, tokens, grad_out)
    packed = pack_weights(a, gate_w, up_w, down_w)
    weights = [packed[0]] + [shift(packed[d], True, d) for d in range(1, SIDE)]

    blocks = unfold(a, exchange(sent, experts), weights[1:])
    blocks = [blocks[0]] + [shift(blocks[d], True, d) for d in range(1, SIDE)]
    head, tail = line_up(a, blocks)
    after_head, before_tail = shift(head, False, 1), shift(tail, False, -1)
    up, down = join(after_head, tail, before_tail, head)
    early = [head, tail, after_head, before_tail]
    late = [shift(up, False, 1), shift(down, False, -1)]

    def presums(pieces, after):
        terms = forward(pieces, weights, after)
        return [terms[0]] + [shift(terms[d], True, -d) for d in range(1, SIDE)]

    def spread(acts):
        return [acts] + [shift(acts, True, d) for d in range(1, SIDE)]

    most = presums(early, [])
    first = spread(activate([most]))
    rest = presums(late, [first[0]])
    hidden = [first, spread(activate([rest]))]
    groups = [early, late]

    own_rows, before_rows, after_rows, far_rows = (0, 1), (2, 5), (7, 3), (4, 6)

    def grads_of(d, after):
        return weight_grads(groups, [chunk[d] for chunk in hidden], after)

    across = grads_of(2, [chunk[d] for chunk in hidden for d in (1, 3)])
    (to_far,) = backward(hidden, weights, (far_rows,), BF16, [across])
    to_before, to_after = backward(
        hidden, weights, (before_rows, after_rows), BF16, [to_far]
    )
    (own,) = backward(hidden, weights, (own_rows,), F32, [to_after])
    row_terms = [
        own,
        shift(to_before, False, -1),
        shift(to_after, False, 1),
        shift(to_far, False, 2),
    ]
    *into, mark = unpack(a, (0,), [grads_of(0, [own])], None)
    grads = [grads_of(d, [own]) for d in (1, 3)]
    *into, mark = unpack(a, (2,), [shift(across, True, -2)], into)
    parts = sum_rows(a, row_terms, [mark] + grads)
    returned = [parts[0]] + [shift(parts[d], True, d) for d in range(1, SIDE)]
    grads = hold(grads, returned[1:])
    folded = fold(a, returned)
    grads = [shift(x, True, -d) for d, x in zip((1, 3), grads)]
    grad_tokens = combine(table, exchange(folded, experts))
    *into, _ = unpack(a, (1, 3), grads, into)
    gate_w_grad, up_w_grad, down_w_grad = into
    return (grad_tokens, gate_w_grad[None], up_w_grad[None], down_w_grad[None])


def solution(mesh):
    return jax.shard_map(
        body,
        mesh=mesh,
        in_specs=(
            P(("grp", "dp", "sp"), None),
            P(("grp", "dp", "sp"), None),
            P(("grp", "dp", "sp"), None),
            P(("grp", "dp", "sp"), None),
            P(("grp", "dp", "sp"), None),
            P(("grp", "sp"), None, "dp"),
            P(("grp", "sp"), None, "dp"),
            P(("grp", "sp"), "dp", None),
        ),
        out_specs=(
            P(("grp", "dp", "sp"), None),
            P(("grp", "sp"), None, "dp"),
            P(("grp", "sp"), None, "dp"),
            P(("grp", "sp"), "dp", None),
        ),
        check_vma=False,
    )
```
